256 devices in a mesh: blk: 128 (over y, z, x_hi, core), rep: 2 (over x_lo).
Axes of the slice: x: 4 (x_hi: 2, x_lo: 2; x = x_hi * 2 + x_lo), y: 4, z: 8, core: 2. Of those that a mesh axis runs over, the one named last changes fastest.
Arguments:
- points: float32 [32, 262144], P(None, 'blk'), may hold values from -6 to 6
- inv_length: float32 [32], replicated, may hold values from 0.08 to 0.3
- direction: float32 [32, 262144], P(None, 'blk'), may hold values from -6 to 6
- residual: float32 [32, 262144], P(None, 'blk'), may hold values from -6 to 6
- solution: float32 [32, 262144], P(None, 'blk'), may hold values from -6 to 6
- active: int32 [32], replicated, may hold values 0 or 1
Outputs:
- solution_next: float32 [32, 262144], P(None, 'blk')
- residual_next: float32 [32, 262144], P(None, 'blk')
- direction_next: float32 [32, 262144], P(None, 'blk')
The draws below stay inside these ranges and needn't reach their ends.
All inputs are finite; a program needn't handle non-finite values.
Results may differ from the reference program's by a relative error of at most 0.0001.
Values sent between devices are 32-bit elements; how exact they have to be, the bound alone decides.
No kernel may reach another device: no remote copies, remote signals or barrier semaphores. Data moves between devices by JAX's collectives and lax.ppermute only.
A program may use at most 64 MiB of HBM per device.

```python
import math
import jax
import jax.numpy as jnp
from jax import lax

BLOCK = 2048
DIM = 32
RHS = 32
NBLK = 128
POINTS = 262144
OFFSET = 32


def touch_ends(values, own_key, low, top_value):
    index_at = [jax.random.randint(jax.random.fold_in(own_key, axis), (), 0, length) for axis, length in enumerate(values.shape)]
    main_axis = values.shape.index(max(values.shape))
    beside = index_at[:main_axis] + [(index_at[main_axis] + 1) % values.shape[main_axis]] + index_at[main_axis + 1:]
    return values.at[tuple(index_at)].set(low).at[tuple(beside)].set(top_value)


def block_scale(own_key, dims, shards, smallest, high):
    def one(position, parts):
        heights = jax.random.uniform(jax.random.fold_in(jax.random.fold_in(own_key, 6), position), (parts,), jnp.float32, smallest / len(shards), high / len(shards))
        return jnp.repeat(jnp.exp(heights), dims[position] // parts).reshape((-1,) + (1,) * (len(dims) - position - 1))

    loudness = one(*shards[0])
    for cut in shards[1:]:
        loudness = loudness * one(*cut)
    return loudness


def bell_draw(key, extent, width, most, shards=(), kind=jnp.bfloat16):
    result = jax.random.normal(key, extent, jnp.float32) * width
    if len(shards) > 0:
        result = block_scale(key, extent, shards, -0.22, 0.18) * result
    return jnp.clip(result, min=-most, max=most).astype(kind)


def setup_inputs(seed: int = 0) -> dict:
    seeds = jax.random.split(jax.random.key(seed), 7)
    return {
        "points": bell_draw(seeds[0], (DIM, POINTS), 1.0, 6.0, ((1, 128),), jnp.float32),
        "inv_length": jnp.clip(jnp.exp(jax.random.uniform(seeds[1], (DIM,), jnp.float32, math.log(0.08), math.log(0.3))), 0.08, 0.3),
        "direction": bell_draw(seeds[2], (RHS, POINTS), 1.0, 6.0, ((1, 128),), jnp.float32),
        "residual": bell_draw(seeds[3], (RHS, POINTS), 1.0, 6.0, ((1, 128),), jnp.float32),
        "solution": bell_draw(seeds[4], (RHS, POINTS), 1.0, 6.0, ((1, 128),), jnp.float32),
        "active": touch_ends((jax.random.randint(seeds[5], (RHS,), 0, 4) < 3).astype(jnp.int32), jax.random.fold_in(seeds[5], 1), 0, 1),
    }


ROOT_FIVE = math.sqrt(5.0)
NOISE = 0.5

def matern(left_pts, right_pts):
    cross = lax.dot_general(left_pts, right_pts, (((0,), (0,)), ((), ())), precision=lax.Precision.HIGHEST)
    sq_dist = lax.optimization_barrier(jnp.sum(left_pts * left_pts, 0))[:, None] + lax.optimization_barrier(jnp.sum(right_pts * right_pts, 0))[None, :] - 2.0 * cross
    scaled_dist = ROOT_FIVE * jnp.sqrt(jnp.maximum(sq_dist, 0.0))
    return (1.0 + scaled_dist + scaled_dist * scaled_dist / 3.0) * jnp.exp(-scaled_dist)

def apply_left(vectors, kernel):
    return lax.dot_general(vectors, kernel, (((1,), (1,)), ((), ())), precision=lax.Precision.HIGHEST)

def apply_right(vectors, kernel):
    return jnp.dot(vectors, kernel, precision=lax.Precision.HIGHEST)

def diagonal_term(entries):
    own_pts, own_dir = entries
    return 4.0 * apply_left(own_dir, matern(own_pts, own_pts))

def pair_term(entries):
    own_pts, own_dir, other_pts, other_dir = entries
    kernel = matern(own_pts, other_pts)
    return (apply_left(other_dir, kernel), apply_right(own_dir, kernel))

def reference(points, inv_length, direction, residual, solution, active):
    scaled_pts = points * inv_length[:, None]
    pts_blocks = scaled_pts.reshape(DIM, NBLK, BLOCK).transpose(1, 0, 2)
    dir_blocks = direction.reshape(RHS, NBLK, BLOCK).transpose(1, 0, 2)
    image_blocks = NOISE * dir_blocks + lax.map(diagonal_term, (pts_blocks, dir_blocks))
    for offset_val in (OFFSET, OFFSET + 1):
        other_pts = jnp.roll(pts_blocks, -offset_val, 0)
        other_dir = jnp.roll(dir_blocks, -offset_val, 0)
        near_part, far_part = lax.map(pair_term, (pts_blocks, dir_blocks, other_pts, other_dir))
        image_blocks = image_blocks + near_part + jnp.roll(far_part, offset_val, 0)
    image = image_blocks.transpose(1, 0, 2).reshape(RHS, POINTS)
    norm_old = lax.optimization_barrier(jnp.sum(residual * residual, 1))
    curvature = lax.optimization_barrier(jnp.sum(direction * image, 1))
    live = active.astype(jnp.float32)
    alpha_vals = live * norm_old / curvature
    solution_next = solution + alpha_vals[:, None] * direction
    residual_next = residual - alpha_vals[:, None] * image
    norm_new = lax.optimization_barrier(jnp.sum(residual_next * residual_next, 1))
    updated = residual_next + (norm_new / norm_old)[:, None] * direction
    direction_next = jnp.where(active[:, None] == 1, updated, direction)
    return (solution_next, residual_next, direction_next)
```

```python
import functools
import math

import jax
import jax.numpy as jnp
from jax import lax
from jax.experimental import pallas as pl
from jax.experimental.pallas import tpu as pltpu
from jax.sharding import PartitionSpec as P

F32, BF16 = jnp.float32, jnp.bfloat16
ROOT_FIVE = math.sqrt(5.0)
LOG2_E = 1.4426950408889634
NOISE = 0.5
BLOCK = 2048
DIM = 32
RHS = 32
TILE = 512
STEPS = BLOCK // TILE
DEPTH = 256
AXES = ("blk", "rep")
NT = (((1,), (1,)), ((), ()))


def pieces(value, count):
    out = []
    for _ in range(count):
        head = value.astype(BF16)
        out.append(head)
        value = value - head.astype(F32)
    return out


def norm_rows(points):
    return [part.astype(F32) for part in pieces(jnp.sum(points * points, 0, keepdims=True), 3)]


def left_side(points):
    n = points.shape[1]
    p = pieces(points, 3)
    m = norm_rows(points)
    row = lax.broadcasted_iota(jnp.int32, (16, n), 0)
    tail = jnp.where(row < 6, 1.0, 0.0)
    for i in range(3):
        tail = jnp.where(row == i, m[i], tail)
    rest = jnp.zeros((DEPTH - 6 * DIM - 16, n), BF16)
    return jnp.concatenate([p[0], p[0], p[1], p[1], p[0], p[2], tail.astype(BF16), rest], 0)


def right_side(points):
    n = points.shape[1]
    p = [(-2.0 * part.astype(F32)).astype(BF16) for part in pieces(points, 3)]
    m = norm_rows(points)
    row = lax.broadcasted_iota(jnp.int32, (16, n), 0)
    tail = jnp.where(row < 3, 1.0, 0.0)
    for i in range(3):
        tail = jnp.where(row == 3 + i, m[i], tail)
    rest = jnp.zeros((DEPTH - 6 * DIM - 16, n), BF16)
    return jnp.concatenate([p[0], p[1], p[0], p[1], p[2], p[0], tail.astype(BF16), rest], 0)


def both_pieces(vectors):
    return jnp.concatenate(pieces(vectors, 2), 0)


def matern_tile(left, right):
    sq = jnp.dot(left, right, preferred_element_type=F32)
    sq = jnp.maximum(sq, 1e-30)
    dist = sq * lax.rsqrt(sq)
    kernel = (dist * (dist + 3.0) + 3.0) * jnp.exp2(dist * -LOG2_E)
    head = kernel.astype(BF16)
    return head, (kernel - head.astype(F32)).astype(BF16)


def to_rows(vectors, kernel):
    return sum(lax.dot_general(vectors, k, NT, preferred_element_type=F32) for k in kernel)


def to_columns(vectors, kernel):
    return sum(jnp.dot(vectors, k, preferred_element_type=F32) for k in kernel)


def folded(total, scale):
    return (total[:RHS] + total[RHS:]) * scale


def own_kernel(pts_ref, len_ref, dir_ref, out_ref, left, right, vecs, total):
    points = pts_ref[...] * len_ref[...] * ROOT_FIVE
    left[...] = left_side(points).T
    right[...] = right_side(points)
    vecs[...] = both_pieces(dir_ref[...])
    total[...] = jnp.zeros_like(total)
    half = lax.axis_index("rep")

    def span(index):
        return pl.ds(pl.multiple_of(index * TILE, TILE), TILE)

    def pair(i, j):
        rows, cols = span(i), span(j)
        kernel = matern_tile(left[rows, :], right[:, cols])
        total[:, rows] += to_rows(vecs[:, cols], kernel)
        total[:, cols] += to_columns(vecs[:, rows], kernel)

    for k in range(STEPS // 2):
        i = half * (STEPS // 2) + k
        rows = span(i)
        kernel = matern_tile(left[rows, :], right[:, rows])
        total[:, rows] += to_columns(vecs[:, rows], kernel)
        pair(i, lax.rem(i + 1, STEPS))
    pair(half, half + STEPS // 2)
    out_ref[...] = folded(total[...], 4.0 / 3.0)


def cross_kernel(
    pts_ref, dir_ref, far_pts_ref, far_dir_ref, len_ref, diag_ref, own_ref, back_ref,
    left, right, vecs, far_vecs, own_total, back_total,
):
    scale = len_ref[...]
    left[...] = left_side(pts_ref[...] * scale * ROOT_FIVE).T
    right[...] = right_side(far_pts_ref[...] * scale * ROOT_FIVE)
    vecs[...] = both_pieces(dir_ref[...])
    far_vecs[...] = both_pieces(far_dir_ref[...])
    back_total[...] = jnp.zeros_like(back_total)

    def some_rows(position, carry):
        rows = pl.ds(pl.multiple_of(position * TILE, TILE), TILE)
        part = jnp.zeros((2 * RHS, TILE), F32)
        for c in range(STEPS):
            cols = slice(c * TILE, (c + 1) * TILE)
            kernel = matern_tile(left[rows, :], right[:, cols])
            part = part + to_rows(far_vecs[:, cols], kernel)
            back_total[:, cols] += to_columns(vecs[:, rows], kernel)
        own_total[:, rows] = part
        return carry

    lax.fori_loop(0, STEPS, some_rows, 0)
    own_ref[...] = folded(own_total[...], 1.0 / 3.0) + diag_ref[...]
    back_ref[...] = folded(back_total[...], 1.0 / 3.0)


def sums_kernel(own_ref, other_ref, dir_ref, res_ref, image_ref, sums_ref):
    vecs, res = dir_ref[...], res_ref[...]
    image = (own_ref[...] + other_ref[...]) + NOISE * vecs
    image_ref[...] = image
    lane = lax.broadcasted_iota(jnp.int32, (RHS, 128), 1)
    table = jnp.zeros((RHS, 128), F32)
    for i, (a, b) in enumerate(((res, res), (vecs, image), (res, image), (image, image))):
        table = jnp.where(lane == i, jnp.sum(a * b, 1, keepdims=True), table)
    table = jnp.concatenate([table, jnp.zeros((128 - RHS, 128), F32)], 0)
    sums_ref[...] = table.T[:8]


def update_kernel(sums_ref, active_ref, image_ref, dir_ref, res_ref, sol_ref, sol_out, res_out, dir_out):
    table = jnp.concatenate([sums_ref[...], jnp.zeros((120, 128), F32)], 0).T
    norm_old, curvature = table[:RHS, 0:1], table[:RHS, 1:2]
    res_image, image_image = table[:RHS, 2:3], table[:RHS, 3:4]
    active = active_ref[...]
    alpha = active.astype(F32) * norm_old / curvature
    norm_new = norm_old - 2.0 * alpha * res_image + alpha * alpha * image_image
    vecs = dir_ref[...]
    sol_out[...] = sol_ref[...] + alpha * vecs
    res_next = res_ref[...] - alpha * image_ref[...]
    res_out[...] = res_next
    dir_out[...] = jnp.where(active == 1, res_next + (norm_new / norm_old) * vecs, vecs)


def place(index):
    rep = index % 2
    core = index // 2 % 2
    x_hi = index // 4 % 2
    z = index // 8 % 8
    return index // 64, z, x_hi, core, rep


def index_of(y, z, x_hi, core, rep):
    return (((y % 4 * 8 + z % 8) * 2 + x_hi % 2) * 2 + core) * 2 + rep


def partner_pairs():
    pairs = []
    for index in range(256):
        block, rep = index // 2, index % 2
        if block % 2 == rep:
            pairs.append((index, (block + 32) % 128 * 2 + rep))
        else:
            pairs.append((index, (block - 33) % 128 * 2 + 1 - rep))
    return pairs


def moved(value, change):
    return lax.ppermute(value, AXES, [(i, index_of(*change(*place(i)))) for i in range(256)])


def all_blocks(value):
    value = value + moved(value, lambda y, z, x, c, r: (y, z, x, 1 - c, r))
    value = value + moved(value, lambda y, z, x, c, r: (y, z, 1 - x, c, 1 - r))
    for step in (1, 2, 4):
        value = value + moved(value, lambda y, z, x, c, r: (y, z ^ step, x, c, r))
    for step in (1, 2):
        value = value + moved(value, lambda y, z, x, c, r: (y ^ step, z, x, c, r))
    return value


def call(kernel, outs, scratch=(), name=None):
    vmem = pl.BlockSpec(memory_space=pltpu.VMEM)
    return pl.pallas_call(
        kernel,
        out_shape=tuple(jax.ShapeDtypeStruct(shape, F32) for shape in outs),
        out_specs=(vmem,) * len(outs),
        scratch_shapes=scratch,
        compiler_params=pltpu.CompilerParams(vmem_limit_bytes=40 * 2**20),
        name=name,
    )


def on_device(points, inv_length, direction, residual, solution, active):
    lengths = inv_length.reshape(DIM, 1)
    there = partner_pairs()
    far_pts = lax.ppermute(points, AXES, there)
    far_dir = lax.ppermute(direction, AXES, there)
    whole = (RHS, BLOCK)
    sides = [pltpu.VMEM((BLOCK, DEPTH), BF16), pltpu.VMEM((DEPTH, BLOCK), BF16)]
    two = pltpu.VMEM((2 * RHS, BLOCK), BF16)
    acc = pltpu.VMEM((2 * RHS, BLOCK), F32)
    (diag,) = call(own_kernel, [whole], sides + [two, acc], "own_tile")(points, lengths, direction)
    own, back = call(cross_kernel, [whole, whole], sides + [two, two, acc, acc], "cross_tile")(
        points, direction, far_pts, far_dir, lengths, diag
    )
    own = own + lax.ppermute(back, AXES, [(d, s) for s, d in there])
    other = moved(own, lambda y, z, x, c, r: (y, z, x, c, 1 - r))
    image, sums = call(sums_kernel, [whole, (8, 128)], name="sums")(own, other, direction, residual)
    sums = all_blocks(sums)
    return call(update_kernel, [whole] * 3, name="update")(
        sums, active.reshape(RHS, 1), image, direction, residual, solution
    )


def solution(mesh):
    placed = (P(None, "blk"), P(), P(None, "blk"), P(None, "blk"), P(None, "blk"), P())
    return jax.shard_map(
        on_device,
        mesh=mesh,
        in_specs=placed,
        out_specs=(P(None, "blk"), P(None, "blk"), P(None, "blk")),
        check_vma=False,
    )
```

```python
import functools
import math

import jax
import jax.numpy as jnp
from jax import lax
from jax.experimental import pallas as pl
from jax.experimental.pallas import tpu as pltpu
from jax.sharding import PartitionSpec as P

F32, BF16 = jnp.float32, jnp.bfloat16
ROOT_FIVE = math.sqrt(5.0)
LOG2_E = 1.4426950408889634
NOISE = 0.5
BLOCK = 2048
DIM = 32
RHS = 32
TILE = 512
STEPS = BLOCK // TILE
DEPTH = 256
AXES = ("blk", "rep")
NT = (((1,), (1,)), ((), ()))


def pieces(value, count):
    out = []
    for _ in range(count):
        head = value.astype(BF16)
        out.append(head)
        value = value - head.astype(F32)
    return out


def norm_rows(points):
    return [part.astype(F32) for part in pieces(jnp.sum(points * points, 0, keepdims=True), 3)]


def left_side(points):
    n = points.shape[1]
    p = pieces(points, 3)
    m = norm_rows(points)
    row = lax.broadcasted_iota(jnp.int32, (16, n), 0)
    tail = jnp.where(row < 6, 1.0, 0.0)
    for i in range(3):
        tail = jnp.where(row == i, m[i], tail)
    rest = jnp.zeros((DEPTH - 6 * DIM - 16, n), BF16)
    return jnp.concatenate([p[0], p[0], p[1], p[1], p[0], p[2], tail.astype(BF16), rest], 0)


def right_side(points):
    n = points.shape[1]
    p = [(-2.0 * part.astype(F32)).astype(BF16) for part in pieces(points, 3)]
    m = norm_rows(points)
    row = lax.broadcasted_iota(jnp.int32, (16, n), 0)
    tail = jnp.where(row < 3, 1.0, 0.0)
    for i in range(3):
        tail = jnp.where(row == 3 + i, m[i], tail)
    rest = jnp.zeros((DEPTH - 6 * DIM - 16, n), BF16)
    return jnp.concatenate([p[0], p[1], p[0], p[1], p[2], p[0], tail.astype(BF16), rest], 0)


def both_pieces(vectors):
    return jnp.concatenate(pieces(vectors, 2), 0)


def matern_tile(left, right):
    sq = jnp.dot(left, right, preferred_element_type=F32)
    sq = jnp.maximum(sq, 1e-30)
    dist = sq * lax.rsqrt(sq)
    kernel = (dist * (dist + 3.0) + 3.0) * jnp.exp2(dist * -LOG2_E)
    head = kernel.astype(BF16)
    return head, (kernel - head.astype(F32)).astype(BF16)


def to_rows(vectors, kernel):
    return sum(lax.dot_general(vectors, k, NT, preferred_element_type=F32) for k in kernel)


def to_columns(vectors, kernel):
    return sum(jnp.dot(vectors, k, preferred_element_type=F32) for k in kernel)


def folded(total, scale):
    return (total[:RHS] + total[RHS:]) * scale


def handles_own_block():
    return lax.rem(lax.axis_index("blk"), 2) == lax.axis_index("rep")


def own_kernel(pts_ref, swap_pts_ref, len_ref, dir_ref, swap_dir_ref, out_ref, left, vecs, right, total):
    mine = handles_own_block()
    points = jnp.where(mine, pts_ref[...], swap_pts_ref[...]) * len_ref[...] * ROOT_FIVE
    left[...] = left_side(points).T
    right[...] = right_side(points)
    vecs[...] = both_pieces(jnp.where(mine, dir_ref[...], swap_dir_ref[...]))
    total[...] = jnp.zeros_like(total)
    half = lax.rem(lax.axis_index("blk"), 2)

    def span(index):
        return pl.ds(pl.multiple_of(index * TILE, TILE), TILE)

    def pair(i, j):
        rows, cols = span(i), span(j)
        kernel = matern_tile(left[rows, :], right[:, cols])
        total[:, rows] += to_rows(vecs[:, cols], kernel)
        total[:, cols] += to_columns(vecs[:, rows], kernel)

    for k in range(STEPS // 2):
        i = half * (STEPS // 2) + k
        rows = span(i)
        kernel = matern_tile(left[rows, :], right[:, rows])
        total[:, rows] += to_columns(vecs[:, rows], kernel)
        pair(i, lax.rem(i + 1, STEPS))
    pair(half, half + STEPS // 2)
    out_ref[...] = folded(total[...], 4.0 / 3.0)


def cross_kernel(
    left, vecs, far_pts_ref, far_dir_ref, len_ref, diag_ref, own_ref, back_ref,
    right, far_vecs, own_total, back_total,
):
    right[...] = right_side(far_pts_ref[...] * len_ref[...] * ROOT_FIVE)
    far_vecs[...] = both_pieces(far_dir_ref[...])
    back_total[...] = jnp.zeros_like(back_total)

    def some_rows(position, carry):
        rows = pl.ds(pl.multiple_of(position * TILE, TILE), TILE)
        part = jnp.zeros((2 * RHS, TILE), F32)
        for c in range(STEPS):
            cols = slice(c * TILE, (c + 1) * TILE)
            kernel = matern_tile(left[rows, :], right[:, cols])
            part = part + to_rows(far_vecs[:, cols], kernel)
            back_total[:, cols] += to_columns(vecs[:, rows], kernel)
        own_total[:, rows] = part
        return carry

    lax.fori_loop(0, STEPS, some_rows, 0)
    own_ref[...] = folded(own_total[...], 1.0 / 3.0) + diag_ref[...]
    back_ref[...] = folded(back_total[...], 1.0 / 3.0)


def sums_kernel(own_ref, other_ref, dir_ref, res_ref, image_ref, sums_ref):
    vecs, res = dir_ref[...], res_ref[...]
    product = own_ref[...] + other_ref[...]
    image_ref[...] = product
    image = product + NOISE * vecs
    lane = lax.broadcasted_iota(jnp.int32, (RHS, 128), 1)
    table = jnp.zeros((RHS, 128), F32)
    for i, (a, b) in enumerate(((res, res), (vecs, image), (res, image), (image, image))):
        table = jnp.where(lane == i, jnp.sum(a * b, 1, keepdims=True), table)
    table = jnp.where(handles_own_block(), table, 0.0)
    table = jnp.concatenate([table, jnp.zeros((128 - RHS, 128), F32)], 0)
    sums_ref[...] = table.T[:8]


def update_kernel(
    sums_ref, active_ref, image_ref, other_ref, dir_ref, res_ref, sol_ref, sol_out, res_out, dir_out
):
    table = sums_ref[0]
    for i in range(1, sums_ref.shape[0]):
        table = table + sums_ref[i]
    table = jnp.concatenate([table, jnp.zeros((120, 128), F32)], 0).T
    norm_old, curvature = table[:RHS, 0:1], table[:RHS, 1:2]
    res_image, image_image = table[:RHS, 2:3], table[:RHS, 3:4]
    active = active_ref[...]
    alpha = active.astype(F32) * norm_old / curvature
    norm_new = norm_old - 2.0 * alpha * res_image + alpha * alpha * image_image
    vecs = dir_ref[...]
    image = jnp.where(handles_own_block(), image_ref[...], other_ref[...]) + NOISE * vecs
    sol_out[...] = sol_ref[...] + alpha * vecs
    res_next = res_ref[...] - alpha * image
    res_out[...] = res_next
    dir_out[...] = jnp.where(active == 1, res_next + (norm_new / norm_old) * vecs, vecs)


def permuted(value, change):
    pairs = []
    for index in range(256):
        block, rep = index // 2, index % 2
        to = change(block, block % 2, rep)
        if to is not None:
            pairs.append((index, to[0] % 128 * 2 + to[1]))
    return lax.ppermute(value, AXES, pairs)


def to_partner(block, core, rep):
    if core == rep:
        return block + 32, rep
    return block - 32 - 2 * rep, rep


def to_home(block, core, rep):
    if core == rep:
        return block - 32, rep
    return block + 31 + 4 * rep, 1 - rep


def swap_core(block, core, rep):
    return block ^ 1, rep


def swap_rep(block, core, rep):
    return block, 1 - rep


def swap_near(block, core, rep):
    return block ^ 2, 1 - rep


def to_twin(block, core, rep):
    return (block, 1 - rep) if core == rep else None


def over_y_and_z(value):
    groups = []
    for low in range(8):
        groups.append([high * 8 + low for high in range(32)])
    copies = jnp.broadcast_to(value[None], (32,) + value.shape)
    return lax.all_to_all(copies, AXES, 0, 0, axis_index_groups=groups)


def call(kernel, outs, scratch=(), name=None):
    vmem = pl.BlockSpec(memory_space=pltpu.VMEM)
    return pl.pallas_call(
        kernel,
        out_shape=tuple(jax.ShapeDtypeStruct(*(out if isinstance(out[0], tuple) else (out, F32))) for out in outs),
        out_specs=(vmem,) * len(outs),
        scratch_shapes=scratch,
        compiler_params=pltpu.CompilerParams(vmem_limit_bytes=40 * 2**20),
        name=name,
    )


def on_device(points, inv_length, direction, residual, solution, active):
    lengths = inv_length.reshape(DIM, 1)
    far_pts = permuted(points, to_partner)
    far_dir = permuted(direction, to_partner)
    swap_pts = permuted(points, swap_core)
    swap_dir = permuted(direction, swap_core)
    whole = (RHS, BLOCK)
    side = pltpu.VMEM((DEPTH, BLOCK), BF16)
    two = pltpu.VMEM((2 * RHS, BLOCK), BF16)
    acc = pltpu.VMEM((2 * RHS, BLOCK), F32)
    diag, left, vecs = call(
        own_kernel, [whole, ((BLOCK, DEPTH), BF16), ((2 * RHS, BLOCK), BF16)], [side, acc], "own_tile"
    )(points, swap_pts, lengths, direction, swap_dir)
    own, back = call(cross_kernel, [whole, whole], [side, two, acc, acc], "cross_tile")(
        left, vecs, far_pts, far_dir, lengths, diag
    )
    own = own + permuted(back, to_home)
    other = permuted(own, swap_core)
    product, sums = call(sums_kernel, [whole, (8, 128)], name="sums")(own, other, direction, residual)
    for change in (swap_core, swap_rep, swap_near):
        sums = sums + permuted(sums, change)
    twin = permuted(product, to_twin)
    return call(update_kernel, [whole] * 3, name="update")(
        over_y_and_z(sums), active.reshape(RHS, 1), product, twin, direction, residual, solution
    )


def solution(mesh):
    placed = (P(None, "blk"), P(), P(None, "blk"), P(None, "blk"), P(None, "blk"), P())
    return jax.shard_map(
        on_device,
        mesh=mesh,
        in_specs=placed,
        out_specs=(P(None, "blk"), P(None, "blk"), P(None, "blk")),
        check_vma=False,
    )
```

```python
import functools
import math

import jax
import jax.numpy as jnp
from jax import lax
from jax.experimental import pallas as pl
from jax.experimental.pallas import tpu as pltpu
from jax.sharding import PartitionSpec as P

F32, BF16 = jnp.float32, jnp.bfloat16
ROOT_FIVE = math.sqrt(5.0)
LOG2_E = 1.4426950408889634
NOISE = 0.5
BLOCK = 2048
DIM = 32
RHS = 32
TILE = 512
STEPS = BLOCK // TILE
DEPTH = 256
AXES = ("blk", "rep")
NT = (((1,), (1,)), ((), ()))


def pieces(value, count):
    out = []
    for _ in range(count):
        head = value.astype(BF16)
        out.append(head)
        value = value - head.astype(F32)
    return out


def norm_rows(points):
    return [part.astype(F32) for part in pieces(jnp.sum(points * points, 0, keepdims=True), 3)]


def left_side(points):
    n = points.shape[1]
    p = pieces(points, 3)
    m = norm_rows(points)
    row = lax.broadcasted_iota(jnp.int32, (16, n), 0)
    tail = jnp.where(row < 6, 1.0, 0.0)
    for i in range(3):
        tail = jnp.where(row == i, m[i], tail)
    rest = jnp.zeros((DEPTH - 6 * DIM - 16, n), BF16)
    return jnp.concatenate([p[0], p[0], p[1], p[1], p[0], p[2], tail.astype(BF16), rest], 0)


def right_side(points):
    n = points.shape[1]
    p = [(-2.0 * part.astype(F32)).astype(BF16) for part in pieces(points, 3)]
    m = norm_rows(points)
    row = lax.broadcasted_iota(jnp.int32, (16, n), 0)
    tail = jnp.where(row < 3, 1.0, 0.0)
    for i in range(3):
        tail = jnp.where(row == 3 + i, m[i], tail)
    rest = jnp.zeros((DEPTH - 6 * DIM - 16, n), BF16)
    return jnp.concatenate([p[0], p[1], p[0], p[1], p[2], p[0], tail.astype(BF16), rest], 0)


def both_pieces(vectors):
    return jnp.concatenate(pieces(vectors, 2), 0)


def matern_tile(left, right):
    sq = jnp.dot(left, right, preferred_element_type=F32)
    sq = jnp.maximum(sq, 1e-30)
    dist = sq * lax.rsqrt(sq)
    kernel = (dist * (dist + 3.0) + 3.0) * jnp.exp2(dist * -LOG2_E)
    head = kernel.astype(BF16)
    return head, (kernel - head.astype(F32)).astype(BF16)


def to_rows(vectors, kernel):
    return sum(lax.dot_general(vectors, k, NT, preferred_element_type=F32) for k in kernel)


def to_columns(vectors, kernel):
    return sum(jnp.dot(vectors, k, preferred_element_type=F32) for k in kernel)


def folded(total, scale):
    return (total[:RHS] + total[RHS:]) * scale


def handles_own_block():
    return lax.rem(lax.axis_index("blk"), 2) == lax.axis_index("rep")


def own_kernel(pts_ref, swap_pts_ref, len_ref, dir_ref, swap_dir_ref, out_ref, left, vecs, right, total):
    mine = handles_own_block()
    points = jnp.where(mine, pts_ref[...], swap_pts_ref[...]) * len_ref[...] * ROOT_FIVE
    left[...] = left_side(points).T
    right[...] = right_side(points)
    vecs[...] = both_pieces(jnp.where(mine, dir_ref[...], swap_dir_ref[...]))
    total[...] = jnp.zeros_like(total)
    half = lax.rem(lax.axis_index("blk"), 2)

    def span(index):
        return pl.ds(pl.multiple_of(index * TILE, TILE), TILE)

    def pair(i, j):
        rows, cols = span(i), span(j)
        kernel = matern_tile(left[rows, :], right[:, cols])
        total[:, rows] += to_rows(vecs[:, cols], kernel)
        total[:, cols] += to_columns(vecs[:, rows], kernel)

    for k in range(STEPS // 2):
        i = half * (STEPS // 2) + k
        rows = span(i)
        kernel = matern_tile(left[rows, :], right[:, rows])
        total[:, rows] += to_columns(vecs[:, rows], kernel)
        pair(i, lax.rem(i + 1, STEPS))
    pair(half, half + STEPS // 2)
    out_ref[...] = folded(total[...], 4.0 / 3.0)


def kernel_kernel(left, vecs, far_pts_ref, len_ref, back_ref, head_ref, rest_ref, right, back_total):
    right[...] = right_side(far_pts_ref[...] * len_ref[...] * ROOT_FIVE)
    back_total[...] = jnp.zeros_like(back_total)

    def some_rows(position, carry):
        rows = pl.ds(pl.multiple_of(position * TILE, TILE), TILE)
        for c in range(STEPS):
            cols = slice(c * TILE, (c + 1) * TILE)
            head, rest = matern_tile(left[rows, :], right[:, cols])
            head_ref[rows, cols] = head
            rest_ref[rows, cols] = rest
            back_total[:, cols] += jnp.dot(vecs[:, rows], head, preferred_element_type=F32)
            back_total[:RHS, cols] += jnp.dot(vecs[:RHS, rows], rest, preferred_element_type=F32)
        return carry

    lax.fori_loop(0, STEPS, some_rows, 0)
    back_ref[...] = folded(back_total[...], 1.0 / 3.0)


def product_kernel(head_ref, rest_ref, far_dir_ref, diag_ref, own_ref, far_vecs, total):
    blank = jnp.zeros((128 - 2 * RHS, BLOCK), BF16)
    far_vecs[...] = jnp.concatenate([both_pieces(far_dir_ref[...]), blank], 0).T

    def some_rows(position, carry):
        rows = pl.ds(pl.multiple_of(position * TILE, TILE), TILE)
        total[rows, :] = jnp.dot(head_ref[rows, :], far_vecs[...], preferred_element_type=F32) + jnp.dot(
            rest_ref[rows, :], far_vecs[...], preferred_element_type=F32
        )
        return carry

    lax.fori_loop(0, STEPS, some_rows, 0)
    own_ref[...] = folded(total[...].T[: 2 * RHS], 1.0 / 3.0) + diag_ref[...]


def sums_kernel(
    own_ref, back_ref, other_ref, dir_ref, swap_dir_ref, res_ref, swap_res_ref, product_ref, sums_ref
):
    mine = handles_own_block()
    vecs = jnp.where(mine, dir_ref[...], swap_dir_ref[...])
    res = jnp.where(mine, res_ref[...], swap_res_ref[...])
    product = (own_ref[...] + back_ref[...]) + other_ref[...]
    product_ref[...] = product
    image = product + NOISE * vecs
    lane = lax.broadcasted_iota(jnp.int32, (RHS, 128), 1)
    table = jnp.zeros((RHS, 128), F32)
    for i, (a, b) in enumerate(((res, res), (vecs, image), (res, image), (image, image))):
        table = jnp.where(lane == i, jnp.sum(a * b, 1, keepdims=True), table)
    table = jnp.concatenate([table, jnp.zeros((128 - RHS, 128), F32)], 0).T
    row = jnp.concatenate([table[i : i + 1, :RHS] for i in range(4)], 1)
    sums_ref[...] = jnp.broadcast_to(row[None], sums_ref.shape)


def update_kernel(
    sums_ref, active_ref, image_ref, other_ref, dir_ref, res_ref, sol_ref, sol_out, res_out, dir_out
):
    row = jnp.sum(sums_ref[...], 0)
    table = jnp.concatenate([row[:, i * RHS : (i + 1) * RHS] for i in range(4)], 0)
    table = jnp.concatenate([table, jnp.zeros((4, RHS), F32)], 0)
    table = jnp.concatenate([table, jnp.zeros((8, 128 - RHS), F32)], 1)
    table = jnp.concatenate([table, jnp.zeros((120, 128), F32)], 0).T
    norm_old, curvature = table[:RHS, 0:1], table[:RHS, 1:2]
    res_image, image_image = table[:RHS, 2:3], table[:RHS, 3:4]
    active = active_ref[...]
    alpha = active.astype(F32) * norm_old / curvature
    norm_new = norm_old - 2.0 * alpha * res_image + alpha * alpha * image_image
    vecs = dir_ref[...]
    image = jnp.where(handles_own_block(), image_ref[...], other_ref[...]) + NOISE * vecs
    sol_out[...] = sol_ref[...] + alpha * vecs
    res_next = res_ref[...] - alpha * image
    res_out[...] = res_next
    dir_out[...] = jnp.where(active == 1, res_next + (norm_new / norm_old) * vecs, vecs)


def permuted(value, change):
    pairs = []
    for index in range(256):
        block, rep = index // 2, index % 2
        to = change(block, block % 2, rep)
        if to is not None:
            pairs.append((index, to[0] % 128 * 2 + to[1]))
    return lax.ppermute(value, AXES, pairs)


def to_partner(block, core, rep):
    if core == 0:
        return (block + 32, 0) if rep == 1 else (block - 34, 1)
    return (block + 32, 1) if rep == 1 else (block - 32, 0)


def to_home(block, core, rep):
    if core == rep:
        return block - 32, rep
    return block + 31 + 4 * rep, 1 - rep


def swap_core(block, core, rep):
    return block ^ 1, rep


def to_twin(block, core, rep):
    return (block, 1 - rep) if core == rep else None


def over_chips(value):
    groups = [[block * 2 + rep for block in range(core, 128, 2) for rep in range(2)] for core in range(2)]
    return lax.all_to_all(value, AXES, 0, 0, axis_index_groups=groups)


def call(kernel, outs, scratch=(), name=None):
    vmem = pl.BlockSpec(memory_space=pltpu.VMEM)
    return pl.pallas_call(
        kernel,
        out_shape=tuple(jax.ShapeDtypeStruct(*(out if isinstance(out[0], tuple) else (out, F32))) for out in outs),
        out_specs=(vmem,) * len(outs),
        scratch_shapes=scratch,
        compiler_params=pltpu.CompilerParams(vmem_limit_bytes=28 * 2**20),
        name=name,
    )


def on_device(points, inv_length, direction, residual, solution, active):
    lengths = inv_length.reshape(DIM, 1)
    far_pts = permuted(points, to_partner)
    far_dir = permuted(direction, to_partner)
    swap_pts = permuted(points, swap_core)
    swap_dir = permuted(direction, swap_core)
    swap_res = permuted(residual, swap_core)
    whole = (RHS, BLOCK)
    square = ((BLOCK, BLOCK), BF16)
    side = pltpu.VMEM((DEPTH, BLOCK), BF16)
    acc = pltpu.VMEM((2 * RHS, BLOCK), F32)
    tall = (BLOCK, 128)
    diag, left, vecs = call(
        own_kernel, [whole, ((BLOCK, DEPTH), BF16), ((2 * RHS, BLOCK), BF16)], [side, acc], "own_tile"
    )(points, swap_pts, lengths, direction, swap_dir)
    back, head, rest = call(kernel_kernel, [whole, square, square], [side, acc], "cross_kernel")(
        left, vecs, far_pts, lengths
    )
    back = permuted(back, to_home)
    (own,) = call(product_kernel, [whole], [pltpu.VMEM(tall, BF16), pltpu.VMEM(tall, F32)], "cross_product")(
        head, rest, far_dir, diag
    )
    part = own + back
    other = permuted(part, swap_core)
    product, sums = call(sums_kernel, [whole, (128, 1, 128)], name="sums")(
        own, back, other, direction, swap_dir, residual, swap_res
    )
    twin = permuted(product, to_twin)
    return call(update_kernel, [whole] * 3, name="update")(
        over_chips(sums), active.reshape(RHS, 1), product, twin, direction, residual, solution
    )


def solution(mesh):
    placed = (P(None, "blk"), P(), P(None, "blk"), P(None, "blk"), P(None, "blk"), P())
    return jax.shard_map(
        on_device,
        mesh=mesh,
        in_specs=placed,
        out_specs=(P(None, "blk"), P(None, "blk"), P(None, "blk")),
        check_vma=False,
    )
```

```python
import functools
import math

import jax
import jax.numpy as jnp
from jax import lax
from jax.experimental import pallas as pl
from jax.experimental.pallas import tpu as pltpu
from jax.sharding import PartitionSpec as P

F32, BF16 = jnp.float32, jnp.bfloat16
ROOT_FIVE = math.sqrt(5.0)
LOG2_E = 1.4426950408889634
SCALE = ROOT_FIVE * LOG2_E
SHARE = 1.0 / (3.0 * LOG2_E * LOG2_E)
NOISE = 0.5
BLOCK = 2048
DIM = 32
RHS = 32
TILE = 512
STEPS = BLOCK // TILE
DEPTH = 256
AXES = ("blk", "rep")
NT = (((1,), (1,)), ((), ()))


def pieces(value, count):
    out = []
    for _ in range(count):
        head = value.astype(BF16)
        out.append(head)
        value = value - head.astype(F32)
    return out


def norm_rows(points):
    return [part.astype(F32) for part in pieces(jnp.sum(points * points, 0, keepdims=True), 3)]


def left_side(points):
    n = points.shape[1]
    p = pieces(points, 3)
    m = norm_rows(points)
    row = lax.broadcasted_iota(jnp.int32, (16, n), 0)
    tail = jnp.where(row < 6, 1.0, 0.0)
    for i in range(3):
        tail = jnp.where(row == i, m[i], tail)
    rest = jnp.zeros((DEPTH - 6 * DIM - 16, n), BF16)
    return jnp.concatenate([p[0], p[0], p[1], p[1], p[0], p[2], tail.astype(BF16), rest], 0)


def right_side(points):
    n = points.shape[1]
    p = [(-2.0 * part.astype(F32)).astype(BF16) for part in pieces(points, 3)]
    m = norm_rows(points)
    row = lax.broadcasted_iota(jnp.int32, (16, n), 0)
    tail = jnp.where(row < 3, 1.0, 0.0)
    for i in range(3):
        tail = jnp.where(row == 3 + i, m[i], tail)
    rest = jnp.zeros((DEPTH - 6 * DIM - 16, n), BF16)
    return jnp.concatenate([p[0], p[1], p[0], p[1], p[2], p[0], tail.astype(BF16), rest], 0)


def both_pieces(vectors):
    return jnp.concatenate(pieces(vectors, 2), 0)


def squares(left, right):
    return jnp.maximum(jnp.dot(left, right, preferred_element_type=F32), 1e-30)


def matern(sq):
    dist = sq * lax.rsqrt(sq)
    return (dist * (dist + 3.0 * LOG2_E) + 3.0 * LOG2_E * LOG2_E) * jnp.exp2(-dist)


def halves(kernel):
    head = kernel.astype(BF16)
    return head, (kernel - head.astype(F32)).astype(BF16)


def add_rows(total, rows, vecs, cols, kernel):
    head, rest = kernel
    total[:, rows] += lax.dot_general(vecs[:, cols], head, NT, preferred_element_type=F32)
    total[:RHS, rows] += lax.dot_general(vecs[:RHS, cols], rest, NT, preferred_element_type=F32)


def add_columns(total, cols, vecs, rows, kernel):
    head, rest = kernel
    total[:, cols] += jnp.dot(vecs[:, rows], head, preferred_element_type=F32)
    total[:RHS, cols] += jnp.dot(vecs[:RHS, rows], rest, preferred_element_type=F32)


def span(index):
    return pl.ds(pl.multiple_of(index * TILE, TILE), TILE)


def as_column(row):
    n = row.shape[1]
    square = lax.broadcasted_iota(jnp.int32, (n, n), 0) == lax.broadcasted_iota(jnp.int32, (n, n), 1)
    return jnp.sum(jnp.where(square, row, jnp.zeros_like(row)), 1, keepdims=True)


def folded(total, scale):
    return (total[:RHS] + total[RHS:]) * scale


def handles_own_block():
    return lax.rem(lax.axis_index("blk"), 2) == lax.axis_index("rep")


def own_tiles(left, right, vecs, total, first):
    half = lax.rem(lax.axis_index("blk"), 2)

    def diagonal(i):
        rows = span(i)
        add_columns(total, rows, vecs, rows, halves(matern(squares(left[rows, :], right[:, rows]))))

    def pair(i, j):
        rows, cols = span(i), span(j)
        kernel = halves(matern(squares(left[rows, :], right[:, cols])))
        add_rows(total, rows, vecs, cols, kernel)
        add_columns(total, cols, vecs, rows, kernel)

    i = half * (STEPS // 2)
    if first:
        diagonal(i)
        pair(i, i + 1)
    else:
        diagonal(i + 1)
        pair(i + 1, lax.rem(i + 2, STEPS))
        pair(half, half + STEPS // 2)


def start_kernel(
    pts_ref, swap_pts_ref, len_ref, dir_ref, swap_dir_ref,
    left, right, vecs, total, scale_ref, pts, dirs, lengths, arrived,
):
    copies = [pltpu.make_async_copy(len_ref, lengths, arrived.at[8])]
    for n, (source, target) in enumerate(((pts_ref, pts), (dir_ref, dirs))):
        for k in range(4):
            rows = slice(k * 8, k * 8 + 8)
            copies.append(pltpu.make_async_copy(source.at[rows], target.at[rows], arrived.at[4 * n + k]))
    for copy in copies:
        copy.start()
    mine = handles_own_block()
    total[...] = jnp.zeros_like(total)
    for copy in copies:
        copy.wait()
    scale = as_column(lengths[...]) * SCALE
    scale_ref[...] = jnp.broadcast_to(scale, scale_ref.shape)
    points = jnp.where(mine, pts[...], swap_pts_ref[...]) * scale
    left[...] = left_side(points).T
    right[...] = right_side(points)
    vecs[...] = both_pieces(jnp.where(mine, dirs[...], swap_dir_ref[...]))
    own_tiles(left, right, vecs, total, True)


def kernel_kernel(left, vecs, far_pts_ref, scale_ref, back_ref, kernel_ref, right, total, sq, parts):
    right[...] = right_side(far_pts_ref[...] * scale_ref[:, 0:1])
    total[...] = jnp.zeros_like(total)
    cols = [slice(c * TILE, (c + 1) * TILE) for c in range(STEPS)]

    def distances(r, c):
        sq[c % 2] = squares(left[span(r), :], right[:, cols[c]])

    def product(r, c):
        add_columns(total, cols[c], vecs, span(r), (parts[c % 2, 0], parts[c % 2, 1]))

    distances(0, 0)

    def some_rows(r, carry):
        for c in range(STEPS):
            if c + 1 < STEPS:
                distances(r, c + 1)
            else:
                distances(jnp.minimum(r + 1, STEPS - 1), 0)
            kernel = matern(sq[c % 2])
            kernel_ref[span(r), cols[c]] = kernel
            parts[c % 2, 0], parts[c % 2, 1] = halves(kernel)
            if c > 0:
                product(r, c - 1)
        product(r, STEPS - 1)
        return carry

    lax.fori_loop(0, STEPS, some_rows, 0)
    back_ref[...] = folded(total[...], SHARE)


def product_kernel(kernel_ref, far_dir_ref, left, right, vecs, total_ref, own_ref, far_vecs, tall, total):
    total[...] = total_ref[...]
    own_tiles(left, right, vecs, total, False)
    blank = jnp.zeros((128 - 2 * RHS, BLOCK), BF16)
    far_vecs[...] = jnp.concatenate([both_pieces(far_dir_ref[...]), blank], 0).T

    def some_rows(r, carry):
        head, rest = halves(kernel_ref[span(r), :])
        tall[span(r), :] = jnp.dot(head, far_vecs[...], preferred_element_type=F32) + jnp.dot(
            rest, far_vecs[...], preferred_element_type=F32
        )
        return carry

    lax.fori_loop(0, STEPS, some_rows, 0)
    own_ref[...] = folded(tall[...].T[: 2 * RHS], SHARE) + folded(total[...], 4.0 * SHARE)


def sums_kernel(
    own_ref, back_ref, other_ref, dir_ref, swap_dir_ref, res_ref, swap_res_ref, product_ref, sums_ref
):
    mine = handles_own_block()
    vecs = jnp.where(mine, dir_ref[...], swap_dir_ref[...])
    res = jnp.where(mine, res_ref[...], swap_res_ref[...])
    product = (own_ref[...] + back_ref[...]) + other_ref[...]
    product_ref[...] = product
    image = product + NOISE * vecs
    lane = lax.broadcasted_iota(jnp.int32, (RHS, 128), 1)
    table = jnp.zeros((RHS, 128), F32)
    for i, (a, b) in enumerate(((res, res), (vecs, image), (res, image), (image, image))):
        table = jnp.where(lane == i, jnp.sum(a * b, 1, keepdims=True), table)
    table = jnp.concatenate([table, jnp.zeros((128 - RHS, 128), F32)], 0).T
    row = jnp.concatenate([table[i : i + 1, :RHS] for i in range(4)], 1)
    sums_ref[...] = jnp.broadcast_to(row[None], sums_ref.shape)


def update_kernel(
    sums_ref, active_ref, image_ref, other_ref, dir_ref, res_ref, sol_ref, sol_out, res_out, dir_out
):
    row = jnp.sum(sums_ref[...], 0)
    table = jnp.concatenate([row[:, i * RHS : (i + 1) * RHS] for i in range(4)], 0)
    table = jnp.concatenate([table, jnp.zeros((4, RHS), F32)], 0)
    table = jnp.concatenate([table, jnp.zeros((8, 128 - RHS), F32)], 1)
    table = jnp.concatenate([table, jnp.zeros((120, 128), F32)], 0).T
    norm_old, curvature = table[:RHS, 0:1], table[:RHS, 1:2]
    res_image, image_image = table[:RHS, 2:3], table[:RHS, 3:4]
    active = as_column(active_ref[...])
    alpha = active.astype(F32) * norm_old / curvature
    norm_new = norm_old - 2.0 * alpha * res_image + alpha * alpha * image_image
    vecs = dir_ref[...]
    image = jnp.where(handles_own_block(), image_ref[...], other_ref[...]) + NOISE * vecs
    sol_out[...] = sol_ref[...] + alpha * vecs
    res_next = res_ref[...] - alpha * image
    res_out[...] = res_next
    dir_out[...] = jnp.where(active == 1, res_next + (norm_new / norm_old) * vecs, vecs)


def permuted(value, change):
    pairs = []
    for index in range(256):
        block, rep = index // 2, index % 2
        to = change(block, block % 2, rep)
        if to is not None:
            pairs.append((index, to[0] % 128 * 2 + to[1]))
    return lax.ppermute(value, AXES, pairs)


def to_partner(block, core, rep):
    if core == 0:
        return (block + 32, 0) if rep == 1 else (block - 34, 1)
    return (block + 32, 1) if rep == 1 else (block - 32, 0)


def to_home(block, core, rep):
    if core == rep:
        return block - 32, rep
    return block + 31 + 4 * rep, 1 - rep


def swap_core(block, core, rep):
    return block ^ 1, rep


def to_twin(block, core, rep):
    return (block, 1 - rep) if core == rep else None


def over_chips(value):
    groups = [[block * 2 + rep for block in range(core, 128, 2) for rep in range(2)] for core in range(2)]
    return lax.all_to_all(value, AXES, 0, 0, axis_index_groups=groups)


def call(kernel, outs, ins, scratch=(), name=None):
    vmem = pl.BlockSpec(memory_space=pltpu.VMEM)
    hbm = pl.BlockSpec(memory_space=pltpu.HBM)
    return pl.pallas_call(
        kernel,
        out_shape=tuple(jax.ShapeDtypeStruct(*(out if isinstance(out[0], tuple) else (out, F32))) for out in outs),
        in_specs=[hbm if i == "h" else vmem for i in ins],
        out_specs=(vmem,) * len(outs),
        scratch_shapes=scratch,
        compiler_params=pltpu.CompilerParams(vmem_limit_bytes=28 * 2**20),
        name=name,
    )


def on_device(points, inv_length, direction, residual, solution, active):
    lengths = inv_length.reshape(1, DIM)
    far_pts = permuted(points, to_partner)
    far_dir = permuted(direction, to_partner)
    swap_pts = permuted(points, swap_core)
    swap_dir = permuted(direction, swap_core)
    swap_res = permuted(residual, swap_core)
    whole = (RHS, BLOCK)
    left_shape, right_shape = ((BLOCK, DEPTH), BF16), ((DEPTH, BLOCK), BF16)
    vecs_shape, total_shape = ((2 * RHS, BLOCK), BF16), ((2 * RHS, BLOCK), F32)
    left, right, vecs, total, scale = call(
        start_kernel,
        [left_shape, right_shape, vecs_shape, total_shape, (DIM, 128)],
        "hvhhv",
        [
            pltpu.VMEM(whole, F32),
            pltpu.VMEM(whole, F32),
            pltpu.VMEM((1, DIM), F32),
            pltpu.SemaphoreType.DMA((9,)),
        ],
        "own_start",
    )(points, swap_pts, lengths, direction, swap_dir)
    back, kernel = call(
        kernel_kernel,
        [whole, (BLOCK, BLOCK)],
        "vvvv",
        [
            pltpu.VMEM(*right_shape),
            pltpu.VMEM(*total_shape),
            pltpu.VMEM((2, TILE, TILE), F32),
            pltpu.VMEM((2, 2, TILE, TILE), BF16),
        ],
        "cross_kernel",
    )(left, vecs, far_pts, scale)
    back = permuted(back, to_home)
    tall = (BLOCK, 128)
    (own,) = call(
        product_kernel,
        [whole],
        "vvvvvv",
        [pltpu.VMEM(tall, BF16), pltpu.VMEM(tall, F32), pltpu.VMEM(*total_shape)],
        "cross_product",
    )(kernel, far_dir, left, right, vecs, total)
    part = own + back
    other = permuted(part, swap_core)
    product, sums = call(sums_kernel, [whole, (128, 1, 128)], "vvvvvvv", name="sums")(
        own, back, other, direction, swap_dir, residual, swap_res
    )
    twin = permuted(product, to_twin)
    return call(update_kernel, [whole] * 3, "vvvvvvv", name="update")(
        over_chips(sums), active.reshape(1, RHS), product, twin, direction, residual, solution
    )


def solution(mesh):
    placed = (P(None, "blk"), P(), P(None, "blk"), P(None, "blk"), P(None, "blk"), P())
    return jax.shard_map(
        on_device,
        mesh=mesh,
        in_specs=placed,
        out_specs=(P(None, "blk"), P(None, "blk"), P(None, "blk")),
        check_vma=False,
    )
```

```python
import functools
import math

import jax
import jax.numpy as jnp
from jax import lax
from jax.experimental import pallas as pl
from jax.experimental.pallas import tpu as pltpu
from jax.sharding import PartitionSpec as P

F32, BF16 = jnp.float32, jnp.bfloat16
ROOT_FIVE = math.sqrt(5.0)
LOG2_E = 1.4426950408889634
SCALE = ROOT_FIVE * LOG2_E
SHARE = 1.0 / (3.0 * LOG2_E * LOG2_E)
NOISE = 0.5
BLOCK = 2048
DIM = 32
RHS = 32
TILE = 512
STEPS = BLOCK // TILE
DEPTH = 256
AXES = ("blk", "rep")
NT = (((1,), (1,)), ((), ()))


def pieces(value, count):
    out = []
    for _ in range(count):
        head = value.astype(BF16)
        out.append(head)
        value = value - head.astype(F32)
    return out


def norm_rows(points):
    return [part.astype(F32) for part in pieces(jnp.sum(points * points, 0, keepdims=True), 3)]


def left_side(points):
    n = points.shape[1]
    p = pieces(points, 3)
    m = norm_rows(points)
    row = lax.broadcasted_iota(jnp.int32, (16, n), 0)
    tail = jnp.where(row < 6, 1.0, 0.0)
    for i in range(3):
        tail = jnp.where(row == i, m[i], tail)
    rest = jnp.zeros((DEPTH - 6 * DIM - 16, n), BF16)
    return jnp.concatenate([p[0], p[0], p[1], p[1], p[0], p[2], tail.astype(BF16), rest], 0)


def right_side(points):
    n = points.shape[1]
    p = [(-2.0 * part.astype(F32)).astype(BF16) for part in pieces(points, 3)]
    m = norm_rows(points)
    row = lax.broadcasted_iota(jnp.int32, (16, n), 0)
    tail = jnp.where(row < 3, 1.0, 0.0)
    for i in range(3):
        tail = jnp.where(row == 3 + i, m[i], tail)
    rest = jnp.zeros((DEPTH - 6 * DIM - 16, n), BF16)
    return jnp.concatenate([p[0], p[1], p[0], p[1], p[2], p[0], tail.astype(BF16), rest], 0)


def both_pieces(vectors):
    return jnp.concatenate(pieces(vectors, 2), 0)


def squares(left, right):
    return jnp.maximum(jnp.dot(left, right, preferred_element_type=F32), 1e-30)


def matern(sq):
    dist = sq * lax.rsqrt(sq)
    return (dist * (dist + 3.0 * LOG2_E) + 3.0 * LOG2_E * LOG2_E) * jnp.exp2(-dist)


def halves(kernel):
    head = kernel.astype(BF16)
    return head, (kernel - head.astype(F32)).astype(BF16)


def add_rows(total, rows, vecs, cols, kernel):
    head, rest = kernel
    total[:, rows] += lax.dot_general(vecs[:, cols], head, NT, preferred_element_type=F32)
    total[:RHS, rows] += lax.dot_general(vecs[:RHS, cols], rest, NT, preferred_element_type=F32)


def add_columns(total, cols, vecs, rows, kernel):
    head, rest = kernel
    total[:, cols] += jnp.dot(vecs[:, rows], head, preferred_element_type=F32)
    total[:RHS, cols] += jnp.dot(vecs[:RHS, rows], rest, preferred_element_type=F32)


def span(index):
    return pl.ds(pl.multiple_of(index * TILE, TILE), TILE)


def as_column(row):
    n = row.shape[1]
    square = lax.broadcasted_iota(jnp.int32, (n, n), 0) == lax.broadcasted_iota(jnp.int32, (n, n), 1)
    return jnp.sum(jnp.where(square, row, jnp.zeros_like(row)), 1, keepdims=True)


def folded(total, scale):
    return (total[:RHS] + total[RHS:]) * scale


def handles_own_block():
    return lax.rem(lax.axis_index("blk"), 2) == lax.axis_index("rep")


def waits_longest():
    return jnp.logical_and(lax.rem(lax.axis_index("blk"), 32) == 30, lax.axis_index("rep") == 1)


def own_tiles(left, right, vecs, total, first):
    half = lax.rem(lax.axis_index("blk"), 2)

    def diagonal(i):
        rows = span(i)
        add_columns(total, rows, vecs, rows, halves(matern(squares(left[rows, :], right[:, rows]))))

    def pair(i, j):
        rows, cols = span(i), span(j)
        kernel = halves(matern(squares(left[rows, :], right[:, cols])))
        add_rows(total, rows, vecs, cols, kernel)
        add_columns(total, cols, vecs, rows, kernel)

    i = half * (STEPS // 2)
    if first:
        diagonal(i)
        pair(i, i + 1)
    else:
        diagonal(i + 1)
        pair(i + 1, lax.rem(i + 2, STEPS))
        pair(half, half + STEPS // 2)


def start_kernel(
    pts_ref, swap_pts_ref, len_ref, dir_ref, swap_dir_ref,
    left, right, vecs, total, scale_ref, pts, dirs, lengths, arrived,
):
    copies = [pltpu.make_async_copy(len_ref, lengths, arrived.at[8])]
    for n, (source, target) in enumerate(((pts_ref, pts), (dir_ref, dirs))):
        for k in range(4):
            rows = slice(k * 8, k * 8 + 8)
            copies.append(pltpu.make_async_copy(source.at[rows], target.at[rows], arrived.at[4 * n + k]))
    for copy in copies:
        copy.start()
    mine = handles_own_block()
    total[...] = jnp.zeros_like(total)
    for copy in copies:
        copy.wait()
    scale = as_column(lengths[...]) * SCALE
    scale_ref[...] = jnp.broadcast_to(scale, scale_ref.shape)
    points = jnp.where(mine, pts[...], swap_pts_ref[...]) * scale
    left[...] = left_side(points).T
    right[...] = right_side(points)
    vecs[...] = both_pieces(jnp.where(mine, dirs[...], swap_dir_ref[...]))
    own_tiles(left, right, vecs, total, True)

    @pl.when(waits_longest())
    def _():
        own_tiles(left, right, vecs, total, False)


def kernel_kernel(left, vecs, far_pts_ref, scale_ref, back_ref, kernel_ref, right, total, sq, parts):
    right[...] = right_side(far_pts_ref[...] * scale_ref[:, 0:1])
    total[...] = jnp.zeros_like(total)
    cols = [slice(c * TILE, (c + 1) * TILE) for c in range(STEPS)]

    def distances(r, c):
        sq[c % 2] = squares(left[span(r), :], right[:, cols[c]])

    def product(r, c):
        add_columns(total, cols[c], vecs, span(r), (parts[c % 2, 0], parts[c % 2, 1]))

    distances(0, 0)

    def some_rows(r, carry):
        for c in range(STEPS):
            if c + 1 < STEPS:
                distances(r, c + 1)
            else:
                distances(jnp.minimum(r + 1, STEPS - 1), 0)
            kernel = matern(sq[c % 2])
            kernel_ref[span(r), cols[c]] = kernel
            parts[c % 2, 0], parts[c % 2, 1] = halves(kernel)
            if c > 0:
                product(r, c - 1)
        product(r, STEPS - 1)
        return carry

    lax.fori_loop(0, STEPS, some_rows, 0)
    back_ref[...] = folded(total[...], SHARE)


def product_kernel(kernel_ref, far_dir_ref, left, right, vecs, total_ref, own_ref, far_vecs, tall, total):
    total[...] = total_ref[...]

    @pl.when(jnp.logical_not(waits_longest()))
    def _():
        own_tiles(left, right, vecs, total, False)

    blank = jnp.zeros((128 - 2 * RHS, BLOCK), BF16)
    far_vecs[...] = jnp.concatenate([both_pieces(far_dir_ref[...]), blank], 0).T

    def some_rows(r, carry):
        head, rest = halves(kernel_ref[span(r), :])
        tall[span(r), :] = jnp.dot(head, far_vecs[...], preferred_element_type=F32) + jnp.dot(
            rest, far_vecs[...], preferred_element_type=F32
        )
        return carry

    lax.fori_loop(0, STEPS, some_rows, 0)
    own_ref[...] = folded(tall[...].T[: 2 * RHS], SHARE) + folded(total[...], 4.0 * SHARE)


def sums_kernel(
    own_ref, back_ref, other_ref, dir_ref, swap_dir_ref, res_ref, swap_res_ref, product_ref, sums_ref
):
    mine = handles_own_block()
    vecs = jnp.where(mine, dir_ref[...], swap_dir_ref[...])
    res = jnp.where(mine, res_ref[...], swap_res_ref[...])
    product = (own_ref[...] + back_ref[...]) + other_ref[...]
    product_ref[...] = product
    image = product + NOISE * vecs
    lane = lax.broadcasted_iota(jnp.int32, (RHS, 128), 1)
    table = jnp.zeros((RHS, 128), F32)
    for i, (a, b) in enumerate(((res, res), (vecs, image), (res, image), (image, image))):
        table = jnp.where(lane == i, jnp.sum(a * b, 1, keepdims=True), table)
    table = jnp.concatenate([table, jnp.zeros((128 - RHS, 128), F32)], 0).T
    row = jnp.concatenate([table[i : i + 1, :RHS] for i in range(4)], 1)
    sums_ref[...] = jnp.broadcast_to(row[None], sums_ref.shape)


def update_kernel(
    sums_ref, active_ref, image_ref, other_ref, dir_ref, res_ref, sol_ref,
    sol_out, res_out, dir_out, sol_next, res_next, dir_next, sent,
):
    row = jnp.sum(sums_ref[...], 0)
    table = jnp.concatenate([row[:, i * RHS : (i + 1) * RHS] for i in range(4)], 0)
    table = jnp.concatenate([table, jnp.zeros((4, RHS), F32)], 0)
    table = jnp.concatenate([table, jnp.zeros((8, 128 - RHS), F32)], 1)
    table = jnp.concatenate([table, jnp.zeros((120, 128), F32)], 0).T
    norm_old, curvature = table[:RHS, 0:1], table[:RHS, 1:2]
    res_image, image_image = table[:RHS, 2:3], table[:RHS, 3:4]
    active = as_column(active_ref[...])
    alpha = active.astype(F32) * norm_old / curvature
    norm_new = norm_old - 2.0 * alpha * res_image + alpha * alpha * image_image
    ratio = norm_new / norm_old
    mine = handles_own_block()
    copies = []
    for k in range(4):
        rows = slice(k * 8, k * 8 + 8)
        vecs = dir_ref[rows]
        image = jnp.where(mine, image_ref[rows], other_ref[rows]) + NOISE * vecs
        sol_next[rows] = sol_ref[rows] + alpha[rows] * vecs
        after = res_ref[rows] - alpha[rows] * image
        res_next[rows] = after
        dir_next[rows] = jnp.where(active[rows] == 1, after + ratio[rows] * vecs, vecs)
        for n, (source, target) in enumerate(((sol_next, sol_out), (res_next, res_out), (dir_next, dir_out))):
            copies.append(pltpu.make_async_copy(source.at[rows], target.at[rows], sent.at[3 * k + n]))
            copies[-1].start()
    for copy in copies:
        copy.wait()


def permuted(value, change):
    pairs = []
    for index in range(256):
        block, rep = index // 2, index % 2
        to = change(block, block % 2, rep)
        if to is not None:
            pairs.append((index, to[0] % 128 * 2 + to[1]))
    return lax.ppermute(value, AXES, pairs)


def to_partner(block, core, rep):
    if core == 0:
        return (block + 32, 0) if rep == 1 else (block - 34, 1)
    return (block + 32, 1) if rep == 1 else (block - 32, 0)


def to_home(block, core, rep):
    if core == rep:
        return block - 32, rep
    return block + 31 + 4 * rep, 1 - rep


def swap_core(block, core, rep):
    return block ^ 1, rep


def to_twin(block, core, rep):
    return (block, 1 - rep) if core == rep else None


def over_chips(value):
    groups = [[block * 2 + rep for block in range(core, 128, 2) for rep in range(2)] for core in range(2)]
    return lax.all_to_all(value, AXES, 0, 0, axis_index_groups=groups)


def call(kernel, outs, ins, scratch=(), name=None, out_space=pltpu.VMEM):
    vmem = pl.BlockSpec(memory_space=pltpu.VMEM)
    hbm = pl.BlockSpec(memory_space=pltpu.HBM)
    run = pl.pallas_call(
        kernel,
        out_shape=tuple(jax.ShapeDtypeStruct(*(out if isinstance(out[0], tuple) else (out, F32))) for out in outs),
        in_specs=[hbm if i == "h" else vmem for i in ins],
        out_specs=(pl.BlockSpec(memory_space=out_space),) * len(outs),
        scratch_shapes=scratch,
        compiler_params=pltpu.CompilerParams(vmem_limit_bytes=28 * 2**20),
        name=name,
    )

    def placed(*args):
        return run(*(pltpu.with_memory_space_constraint(a, pltpu.HBM) if i == "h" else a for i, a in zip(ins, args)))

    return placed


def on_device(points, inv_length, direction, residual, solution, active):
    lengths = inv_length.reshape(1, DIM)
    far_pts = permuted(points, to_partner)
    far_dir = permuted(direction, to_partner)
    swap_pts = permuted(points, swap_core)
    swap_dir = permuted(direction, swap_core)
    swap_res = permuted(residual, swap_core)
    whole = (RHS, BLOCK)
    left_shape, right_shape = ((BLOCK, DEPTH), BF16), ((DEPTH, BLOCK), BF16)
    vecs_shape, total_shape = ((2 * RHS, BLOCK), BF16), ((2 * RHS, BLOCK), F32)
    left, right, vecs, total, scale = call(
        start_kernel,
        [left_shape, right_shape, vecs_shape, total_shape, (DIM, 128)],
        "hvhhv",
        [
            pltpu.VMEM(whole, F32),
            pltpu.VMEM(whole, F32),
            pltpu.VMEM((1, DIM), F32),
            pltpu.SemaphoreType.DMA((9,)),
        ],
        "own_start",
    )(points, swap_pts, lengths, direction, swap_dir)
    back, kernel = call(
        kernel_kernel,
        [whole, (BLOCK, BLOCK)],
        "vvvv",
        [
            pltpu.VMEM(*right_shape),
            pltpu.VMEM(*total_shape),
            pltpu.VMEM((2, TILE, TILE), F32),
            pltpu.VMEM((2, 2, TILE, TILE), BF16),
        ],
        "cross_kernel",
    )(left, vecs, far_pts, scale)
    back = permuted(back, to_home)
    tall = (BLOCK, 128)
    (own,) = call(
        product_kernel,
        [whole],
        "vvvvvv",
        [pltpu.VMEM(tall, BF16), pltpu.VMEM(tall, F32), pltpu.VMEM(*total_shape)],
        "cross_product",
    )(kernel, far_dir, left, right, vecs, total)
    part = own + back
    other = permuted(part, swap_core)
    product, sums = call(sums_kernel, [whole, (128, 1, 128)], "vvvvvvv", name="sums")(
        own, back, other, direction, swap_dir, residual, swap_res
    )
    twin = permuted(product, to_twin)
    return call(
        update_kernel,
        [whole] * 3,
        "vvvvvvv",
        [pltpu.VMEM(whole, F32)] * 3 + [pltpu.SemaphoreType.DMA((12,))],
        "update",
        pltpu.HBM,
    )(
        over_chips(sums), active.reshape(1, RHS), product, twin, direction, residual, solution
    )


def solution(mesh):
    placed = (P(None, "blk"), P(), P(None, "blk"), P(None, "blk"), P(None, "blk"), P())
    return jax.shard_map(
        on_device,
        mesh=mesh,
        in_specs=placed,
        out_specs=(P(None, "blk"), P(None, "blk"), P(None, "blk")),
        check_vma=False,
    )
```

```python
import functools
import math

import jax
import jax.numpy as jnp
from jax import lax
from jax.experimental import pallas as pl
from jax.experimental.pallas import tpu as pltpu
from jax.sharding import PartitionSpec as P

F32, BF16 = jnp.float32, jnp.bfloat16
ROOT_FIVE = math.sqrt(5.0)
LOG2_E = 1.4426950408889634
SCALE = ROOT_FIVE * LOG2_E
SHARE = 1.0 / (3.0 * LOG2_E * LOG2_E)
NOISE = 0.5
BLOCK = 2048
DIM = 32
RHS = 32
TILE = 512
STEPS = BLOCK // TILE
DEPTH = 256
AXES = ("blk", "rep")
NT = (((1,), (1,)), ((), ()))


def pieces(value, count):
    out = []
    for _ in range(count):
        head = value.astype(BF16)
        out.append(head)
        value = value - head.astype(F32)
    return out


def norm_rows(points):
    return [part.astype(F32) for part in pieces(jnp.sum(points * points, 0, keepdims=True), 3)]


def left_side(points):
    n = points.shape[1]
    p = pieces(points, 3)
    m = norm_rows(points)
    row = lax.broadcasted_iota(jnp.int32, (16, n), 0)
    tail = jnp.where(row < 6, 1.0, 0.0)
    for i in range(3):
        tail = jnp.where(row == i, m[i], tail)
    rest = jnp.zeros((DEPTH - 6 * DIM - 16, n), BF16)
    return jnp.concatenate([p[0], p[0], p[1], p[1], p[0], p[2], tail.astype(BF16), rest], 0)


def right_side(points):
    n = points.shape[1]
    p = [(-2.0 * part.astype(F32)).astype(BF16) for part in pieces(points, 3)]
    m = norm_rows(points)
    row = lax.broadcasted_iota(jnp.int32, (16, n), 0)
    tail = jnp.where(row < 3, 1.0, 0.0)
    for i in range(3):
        tail = jnp.where(row == 3 + i, m[i], tail)
    rest = jnp.zeros((DEPTH - 6 * DIM - 16, n), BF16)
    return jnp.concatenate([p[0], p[1], p[0], p[1], p[2], p[0], tail.astype(BF16), rest], 0)


def both_pieces(vectors):
    return jnp.concatenate(pieces(vectors, 2), 0)


def squares(left, right):
    return jnp.maximum(jnp.dot(left, right, preferred_element_type=F32), 1e-30)


def matern(sq):
    dist = sq * lax.rsqrt(sq)
    return (dist * (dist + 3.0 * LOG2_E) + 3.0 * LOG2_E * LOG2_E) * jnp.exp2(-dist)


def halves(kernel):
    head = kernel.astype(BF16)
    return head, (kernel - head.astype(F32)).astype(BF16)


def add_rows(total, rows, vecs, cols, kernel):
    head, rest = kernel
    total[:, rows] += lax.dot_general(vecs[:, cols], head, NT, preferred_element_type=F32)
    total[:RHS, rows] += lax.dot_general(vecs[:RHS, cols], rest, NT, preferred_element_type=F32)


def add_columns(total, cols, vecs, rows, kernel):
    head, rest = kernel
    total[:, cols] += jnp.dot(vecs[:, rows], head, preferred_element_type=F32)
    total[:RHS, cols] += jnp.dot(vecs[:RHS, rows], rest, preferred_element_type=F32)


def span(index):
    return pl.ds(pl.multiple_of(index * TILE, TILE), TILE)


def as_column(row):
    n = row.shape[1]
    square = lax.broadcasted_iota(jnp.int32, (n, n), 0) == lax.broadcasted_iota(jnp.int32, (n, n), 1)
    return jnp.sum(jnp.where(square, row, jnp.zeros_like(row)), 1, keepdims=True)


def folded(total, scale):
    return (total[:RHS] + total[RHS:]) * scale


def handles_own_block():
    return lax.rem(lax.axis_index("blk"), 2) == lax.axis_index("rep")


def waits_longest():
    return jnp.logical_and(lax.rem(lax.axis_index("blk"), 4) == 2, lax.axis_index("rep") == 1)


def own_tiles(left, right, vecs, total, first):
    half = lax.rem(lax.axis_index("blk"), 2)

    def diagonal(i):
        rows = span(i)
        add_columns(total, rows, vecs, rows, halves(matern(squares(left[rows, :], right[:, rows]))))

    def pair(i, j):
        rows, cols = span(i), span(j)
        kernel = halves(matern(squares(left[rows, :], right[:, cols])))
        add_rows(total, rows, vecs, cols, kernel)
        add_columns(total, cols, vecs, rows, kernel)

    i = half * (STEPS // 2)
    if first:
        diagonal(i)
        pair(i, i + 1)
    else:
        diagonal(i + 1)
        pair(i + 1, lax.rem(i + 2, STEPS))
        pair(half, half + STEPS // 2)


def start_kernel(
    pts_ref, swap_pts_ref, len_ref, dir_ref, swap_dir_ref,
    left, right, vecs, total, scale_ref, pts, dirs, lengths, arrived,
):
    copies = [pltpu.make_async_copy(len_ref, lengths, arrived.at[8])]
    for n, (source, target) in enumerate(((pts_ref, pts), (dir_ref, dirs))):
        for k in range(4):
            rows = slice(k * 8, k * 8 + 8)
            copies.append(pltpu.make_async_copy(source.at[rows], target.at[rows], arrived.at[4 * n + k]))
    for copy in copies:
        copy.start()
    mine = handles_own_block()
    total[...] = jnp.zeros_like(total)
    for copy in copies:
        copy.wait()
    scale = as_column(lengths[...]) * SCALE
    scale_ref[...] = jnp.broadcast_to(scale, scale_ref.shape)
    points = jnp.where(mine, pts[...], swap_pts_ref[...]) * scale
    left[...] = left_side(points).T
    right[...] = right_side(points)
    vecs[...] = both_pieces(jnp.where(mine, dirs[...], swap_dir_ref[...]))
    own_tiles(left, right, vecs, total, True)


def early_kernel(left, right, vecs, total_in, scale_in, total, scale):
    total[...] = total_in[...]
    scale[...] = scale_in[...]

    @pl.when(waits_longest())
    def _():
        own_tiles(left, right, vecs, total, False)


def late_kernel(left, right, vecs, total_in, back_in, total, back):
    total[...] = total_in[...]
    back[...] = back_in[...]

    @pl.when(jnp.logical_not(waits_longest()))
    def _():
        own_tiles(left, right, vecs, total, False)


def kernel_kernel(left, vecs, far_pts_ref, scale_ref, back_ref, kernel_ref, right, total, sq, parts):
    right[...] = right_side(far_pts_ref[...] * scale_ref[:, 0:1])
    total[...] = jnp.zeros_like(total)
    cols = [slice(c * TILE, (c + 1) * TILE) for c in range(STEPS)]

    def distances(r, c):
        sq[c % 2] = squares(left[span(r), :], right[:, cols[c]])

    def product(r, c):
        add_columns(total, cols[c], vecs, span(r), (parts[c % 2, 0], parts[c % 2, 1]))

    distances(0, 0)

    def some_rows(r, carry):
        for c in range(STEPS):
            if c + 1 < STEPS:
                distances(r, c + 1)
            else:
                distances(jnp.minimum(r + 1, STEPS - 1), 0)
            kernel = matern(sq[c % 2])
            kernel_ref[span(r), cols[c]] = kernel
            parts[c % 2, 0], parts[c % 2, 1] = halves(kernel)
            if c > 0:
                product(r, c - 1)
        product(r, STEPS - 1)
        return carry

    lax.fori_loop(0, STEPS, some_rows, 0)
    back_ref[...] = folded(total[...], SHARE)


def product_kernel(kernel_ref, far_dir_ref, total_ref, own_ref, far_vecs, tall):
    blank = jnp.zeros((128 - 2 * RHS, BLOCK), BF16)
    far_vecs[...] = jnp.concatenate([both_pieces(far_dir_ref[...]), blank], 0).T

    def some_rows(r, carry):
        head, rest = halves(kernel_ref[span(r), :])
        tall[span(r), :] = jnp.dot(head, far_vecs[...], preferred_element_type=F32) + jnp.dot(
            rest, far_vecs[...], preferred_element_type=F32
        )
        return carry

    lax.fori_loop(0, STEPS, some_rows, 0)
    own_ref[...] = folded(tall[...].T[: 2 * RHS], SHARE) + folded(total_ref[...], 4.0 * SHARE)


def sums_kernel(
    own_ref, back_ref, other_ref, dir_ref, swap_dir_ref, res_ref, swap_res_ref, product_ref, sums_ref
):
    mine = handles_own_block()
    vecs = jnp.where(mine, dir_ref[...], swap_dir_ref[...])
    res = jnp.where(mine, res_ref[...], swap_res_ref[...])
    product = (own_ref[...] + back_ref[...]) + other_ref[...]
    product_ref[...] = product
    image = product + NOISE * vecs
    lane = lax.broadcasted_iota(jnp.int32, (RHS, 128), 1)
    table = jnp.zeros((RHS, 128), F32)
    for i, (a, b) in enumerate(((res, res), (vecs, image), (res, image), (image, image))):
        table = jnp.where(lane == i, jnp.sum(a * b, 1, keepdims=True), table)
    table = jnp.concatenate([table, jnp.zeros((128 - RHS, 128), F32)], 0).T
    row = jnp.concatenate([table[i : i + 1, :RHS] for i in range(4)], 1)
    sums_ref[...] = jnp.broadcast_to(row[None], sums_ref.shape)


def update_kernel(
    sums_ref, active_ref, image_ref, other_ref, dir_ref, res_ref, sol_ref,
    sol_out, res_out, dir_out, sol_next, res_next, dir_next, sent,
):
    row = jnp.sum(sums_ref[...], 0)
    table = jnp.concatenate([row[:, i * RHS : (i + 1) * RHS] for i in range(4)], 0)
    table = jnp.concatenate([table, jnp.zeros((4, RHS), F32)], 0)
    table = jnp.concatenate([table, jnp.zeros((8, 128 - RHS), F32)], 1)
    table = jnp.concatenate([table, jnp.zeros((120, 128), F32)], 0).T
    norm_old, curvature = table[:RHS, 0:1], table[:RHS, 1:2]
    res_image, image_image = table[:RHS, 2:3], table[:RHS, 3:4]
    active = as_column(active_ref[...])
    alpha = active.astype(F32) * norm_old / curvature
    norm_new = norm_old - 2.0 * alpha * res_image + alpha * alpha * image_image
    ratio = norm_new / norm_old
    mine = handles_own_block()
    copies = []
    for k in range(4):
        rows = slice(k * 8, k * 8 + 8)
        vecs = dir_ref[rows]
        image = jnp.where(mine, image_ref[rows], other_ref[rows]) + NOISE * vecs
        sol_next[rows] = sol_ref[rows] + alpha[rows] * vecs
        after = res_ref[rows] - alpha[rows] * image
        res_next[rows] = after
        dir_next[rows] = jnp.where(active[rows] == 1, after + ratio[rows] * vecs, vecs)
        for n, (source, target) in enumerate(((sol_next, sol_out), (res_next, res_out), (dir_next, dir_out))):
            copies.append(pltpu.make_async_copy(source.at[rows], target.at[rows], sent.at[3 * k + n]))
            copies[-1].start()
    for copy in copies:
        copy.wait()


def permuted(value, change):
    pairs = []
    for index in range(256):
        block, rep = index // 2, index % 2
        to = change(block, block % 2, rep)
        if to is not None:
            pairs.append((index, to[0] % 128 * 2 + to[1]))
    return lax.ppermute(value, AXES, pairs)


def to_partner(block, core, rep):
    if core == 0:
        return (block + 32, 0) if rep == 1 else (block - 34, 1)
    return (block + 32, 1) if rep == 1 else (block - 32, 0)


def to_home(block, core, rep):
    if core == rep:
        return block - 32, rep
    return block + 31 + 4 * rep, 1 - rep


def swap_core(block, core, rep):
    return block ^ 1, rep


def to_twin(block, core, rep):
    return (block, 1 - rep) if core == rep else None


def over_chips(value):
    groups = [[block * 2 + rep for block in range(core, 128, 2) for rep in range(2)] for core in range(2)]
    return lax.all_to_all(value, AXES, 0, 0, axis_index_groups=groups)


def call(kernel, outs, ins, scratch=(), name=None, out_space=pltpu.VMEM):
    vmem = pl.BlockSpec(memory_space=pltpu.VMEM)
    hbm = pl.BlockSpec(memory_space=pltpu.HBM)
    run = pl.pallas_call(
        kernel,
        out_shape=tuple(jax.ShapeDtypeStruct(*(out if isinstance(out[0], tuple) else (out, F32))) for out in outs),
        in_specs=[hbm if i == "h" else vmem for i in ins],
        out_specs=(pl.BlockSpec(memory_space=out_space),) * len(outs),
        scratch_shapes=scratch,
        compiler_params=pltpu.CompilerParams(vmem_limit_bytes=28 * 2**20),
        name=name,
    )

    def placed(*args):
        return run(*(pltpu.with_memory_space_constraint(a, pltpu.HBM) if i == "h" else a for i, a in zip(ins, args)))

    return placed


def on_device(points, inv_length, direction, residual, solution, active):
    lengths = inv_length.reshape(1, DIM)
    far_pts = permuted(points, to_partner)
    swap_pts = permuted(points, swap_core)
    swap_dir = permuted(direction, swap_core)
    swap_res = permuted(residual, swap_core)
    whole = (RHS, BLOCK)
    left_shape, right_shape = ((BLOCK, DEPTH), BF16), ((DEPTH, BLOCK), BF16)
    vecs_shape, total_shape = ((2 * RHS, BLOCK), BF16), ((2 * RHS, BLOCK), F32)
    left, right, vecs, total, scale = call(
        start_kernel,
        [left_shape, right_shape, vecs_shape, total_shape, (DIM, 128)],
        "hvhhv",
        [
            pltpu.VMEM(whole, F32),
            pltpu.VMEM(whole, F32),
            pltpu.VMEM((1, DIM), F32),
            pltpu.SemaphoreType.DMA((9,)),
        ],
        "own_start",
    )(points, swap_pts, lengths, direction, swap_dir)
    later, scale = lax.optimization_barrier((direction, scale))
    far_dir = permuted(later, to_partner)
    total, scale = call(
        early_kernel, [total_shape, (DIM, 128)], "vvvvv", name="own_early"
    )(left, right, vecs, total, scale)
    back, kernel = call(
        kernel_kernel,
        [whole, (BLOCK, BLOCK)],
        "vvvv",
        [
            pltpu.VMEM(*right_shape),
            pltpu.VMEM(*total_shape),
            pltpu.VMEM((2, TILE, TILE), F32),
            pltpu.VMEM((2, 2, TILE, TILE), BF16),
        ],
        "cross_kernel",
    )(left, vecs, far_pts, scale)
    total, back = call(late_kernel, [total_shape, whole], "vvvvv", name="own_late")(
        left, right, vecs, total, back
    )
    back = permuted(back, to_home)
    tall = (BLOCK, 128)
    (own,) = call(
        product_kernel,
        [whole],
        "vvv",
        [pltpu.VMEM(tall, BF16), pltpu.VMEM(tall, F32)],
        "cross_product",
    )(kernel, far_dir, total)
    part = own + back
    other = permuted(part, swap_core)
    product, sums = call(sums_kernel, [whole, (128, 1, 128)], "vvvvvvv", name="sums")(
        own, back, other, direction, swap_dir, residual, swap_res
    )
    twin = permuted(product, to_twin)
    return call(
        update_kernel,
        [whole] * 3,
        "vvvvvvv",
        [pltpu.VMEM(whole, F32)] * 3 + [pltpu.SemaphoreType.DMA((12,))],
        "update",
        pltpu.HBM,
    )(
        over_chips(sums), active.reshape(1, RHS), product, twin, direction, residual, solution
    )


def solution(mesh):
    placed = (P(None, "blk"), P(), P(None, "blk"), P(None, "blk"), P(None, "blk"), P())
    return jax.shard_map(
        on_device,
        mesh=mesh,
        in_specs=placed,
        out_specs=(P(None, "blk"), P(None, "blk"), P(None, "blk")),
        check_vma=False,
    )
```

```python
import functools
import math

import jax
import jax.numpy as jnp
from jax import lax
from jax.experimental import pallas as pl
from jax.experimental.pallas import tpu as pltpu
from jax.sharding import PartitionSpec as P

F32, BF16, F8 = jnp.float32, jnp.bfloat16, jnp.float8_e4m3fn
ROOT_FIVE = math.sqrt(5.0)
LOG2_E = 1.4426950408889634
SCALE = ROOT_FIVE * LOG2_E
SHARE = 1.0 / (3.0 * LOG2_E * LOG2_E)
NOISE = 0.5
BLOCK = 2048
DIM = 32
RHS = 32
TILE = 512
STEPS = BLOCK // TILE
WIDTH = 256
ACROSS = BLOCK // WIDTH
REST_SCALE = 2.0**14
LOW_SCALE = 2.0**4
DEPTH = 256
AXES = ("blk", "rep")
NT = (((1,), (1,)), ((), ()))


def pieces(value, count):
    out = []
    for _ in range(count):
        head = value.astype(BF16)
        out.append(head)
        value = value - head.astype(F32)
    return out


def norm_rows(points):
    return [part.astype(F32) for part in pieces(jnp.sum(points * points, 0, keepdims=True), 3)]


def left_side(points):
    n = points.shape[1]
    p = pieces(points, 3)
    m = norm_rows(points)
    row = lax.broadcasted_iota(jnp.int32, (16, n), 0)
    tail = jnp.where(row < 6, 1.0, 0.0)
    for i in range(3):
        tail = jnp.where(row == i, m[i], tail)
    rest = jnp.zeros((DEPTH - 6 * DIM - 16, n), BF16)
    return jnp.concatenate([p[0], p[0], p[1], p[1], p[0], p[2], tail.astype(BF16), rest], 0)


def right_side(points):
    n = points.shape[1]
    p = [(-2.0 * part.astype(F32)).astype(BF16) for part in pieces(points, 3)]
    m = norm_rows(points)
    row = lax.broadcasted_iota(jnp.int32, (16, n), 0)
    tail = jnp.where(row < 3, 1.0, 0.0)
    for i in range(3):
        tail = jnp.where(row == 3 + i, m[i], tail)
    rest = jnp.zeros((DEPTH - 6 * DIM - 16, n), BF16)
    return jnp.concatenate([p[0], p[1], p[0], p[1], p[2], p[0], tail.astype(BF16), rest], 0)


def both_pieces(vectors):
    return jnp.concatenate(pieces(vectors, 2), 0)


def squares(left, right):
    return jnp.maximum(jnp.dot(left, right, preferred_element_type=F32), 1e-30)


def matern(sq):
    dist = sq * lax.rsqrt(sq)
    return (dist * (dist + 3.0 * LOG2_E) + 3.0 * LOG2_E * LOG2_E) * jnp.exp2(-dist)


def halves(kernel):
    head = kernel.astype(BF16)
    return head, (kernel - head.astype(F32)).astype(BF16)


def add_rows(total, rows, vecs, cols, kernel):
    head, rest = kernel
    total[:, rows] += lax.dot_general(vecs[:, cols], head, NT, preferred_element_type=F32)
    total[:RHS, rows] += lax.dot_general(vecs[:RHS, cols], rest, NT, preferred_element_type=F32)


def add_columns(total, cols, vecs, rows, kernel):
    head, rest = kernel
    total[:, cols] += jnp.dot(vecs[:, rows], head, preferred_element_type=F32)
    total[:RHS, cols] += jnp.dot(vecs[:RHS, rows], rest, preferred_element_type=F32)


def span(index):
    return pl.ds(pl.multiple_of(index * TILE, TILE), TILE)


def as_column(row):
    n = row.shape[1]
    square = lax.broadcasted_iota(jnp.int32, (n, n), 0) == lax.broadcasted_iota(jnp.int32, (n, n), 1)
    return jnp.sum(jnp.where(square, row, jnp.zeros_like(row)), 1, keepdims=True)


def folded(total, scale):
    return (total[:RHS] + total[RHS:]) * scale


def handles_own_block():
    return lax.rem(lax.axis_index("blk"), 2) == lax.axis_index("rep")


def waits_longest():
    return jnp.logical_and(lax.rem(lax.axis_index("blk"), 2) == 0, lax.axis_index("rep") == 1)


def own_tiles(left, right, vecs, total, first):
    half = lax.rem(lax.axis_index("blk"), 2)

    def diagonal(i):
        rows = span(i)
        add_columns(total, rows, vecs, rows, halves(matern(squares(left[rows, :], right[:, rows]))))

    def pair(i, j):
        rows, cols = span(i), span(j)
        kernel = halves(matern(squares(left[rows, :], right[:, cols])))
        add_rows(total, rows, vecs, cols, kernel)
        add_columns(total, cols, vecs, rows, kernel)

    i = half * (STEPS // 2)
    if first:
        diagonal(i)
        pair(i, i + 1)
    else:
        diagonal(i + 1)
        pair(i + 1, lax.rem(i + 2, STEPS))
        pair(half, half + STEPS // 2)


def start_kernel(
    pts_ref, swap_pts_ref, len_ref, dir_ref, swap_dir_ref,
    left, right, vecs, total, scale_ref, pts, dirs, lengths, arrived,
):
    copies = [pltpu.make_async_copy(len_ref, lengths, arrived.at[8])]
    for n, (source, target) in enumerate(((pts_ref, pts), (dir_ref, dirs))):
        for k in range(4):
            rows = slice(k * 8, k * 8 + 8)
            copies.append(pltpu.make_async_copy(source.at[rows], target.at[rows], arrived.at[4 * n + k]))
    for copy in copies:
        copy.start()
    mine = handles_own_block()
    total[...] = jnp.zeros_like(total)
    for copy in copies:
        copy.wait()
    scale = as_column(lengths[...]) * SCALE
    scale_ref[...] = jnp.broadcast_to(scale, scale_ref.shape)
    points = jnp.where(mine, pts[...], swap_pts_ref[...]) * scale
    left[...] = left_side(points).T
    right[...] = right_side(points)
    vecs[...] = both_pieces(jnp.where(mine, dirs[...], swap_dir_ref[...]))
    own_tiles(left, right, vecs, total, True)


def early_kernel(left, right, vecs, total_in, scale_in, total, scale):
    total[...] = total_in[...]
    scale[...] = scale_in[...]

    @pl.when(waits_longest())
    def _():
        own_tiles(left, right, vecs, total, False)


def late_kernel(left, right, vecs, total_in, back_in, total, back):
    total[...] = total_in[...]
    back[...] = back_in[...]

    @pl.when(jnp.logical_not(waits_longest()))
    def _():
        own_tiles(left, right, vecs, total, False)


def kernel_kernel(left, vecs, far_pts_ref, scale_ref, back_ref, kernel_ref, right, total, sq, parts):
    right[...] = right_side(far_pts_ref[...] * scale_ref[:, 0:1])
    total[...] = jnp.zeros_like(total)
    cols = [slice(c * WIDTH, (c + 1) * WIDTH) for c in range(ACROSS)]

    def distances(r, c):
        sq[c % 2] = squares(left[span(r), :], right[:, cols[c]])

    def product(r, c):
        add_columns(total, cols[c], vecs, span(r), (parts[c % 2, 0], parts[c % 2, 1]))

    distances(0, 0)

    def some_rows(r, carry):
        for c in range(ACROSS):
            if c + 1 < ACROSS:
                distances(r, c + 1)
            else:
                distances(jnp.minimum(r + 1, STEPS - 1), 0)
            kernel = matern(sq[c % 2])
            kernel_ref[span(r), cols[c]] = kernel
            parts[c % 2, 0], parts[c % 2, 1] = halves(kernel)
            if c > 0:
                product(r, c - 1)
        product(r, ACROSS - 1)
        return carry

    lax.fori_loop(0, STEPS, some_rows, 0)
    back_ref[...] = folded(total[...], SHARE)


def product_kernel(kernel_ref, far_dir_ref, total_ref, own_ref, far_vecs, far_coarse, tall):
    vecs = far_dir_ref[...]
    coarse = vecs.astype(F8).astype(F32)
    fine = ((vecs - coarse) * LOW_SCALE).astype(F8).astype(F32)
    columns = jnp.concatenate([part.astype(F32) for part in pieces(vecs, 2)] + [coarse, fine], 0).T
    far_vecs[...] = columns.astype(BF16)
    far_coarse[...] = columns.astype(F8)
    from_head = lax.broadcasted_iota(jnp.int32, (TILE, 128), 1) < 2 * RHS

    def some_rows(r, carry):
        kernel = kernel_ref[span(r), :]
        head = kernel.astype(BF16)
        rest = ((kernel - head.astype(F32)) * REST_SCALE).astype(F8)
        tall[span(r), :] = jnp.where(
            from_head,
            jnp.dot(head, far_vecs[...], preferred_element_type=F32),
            jnp.dot(rest, far_coarse[...], preferred_element_type=F32),
        )
        return carry

    lax.fori_loop(0, STEPS, some_rows, 0)
    wide = tall[...].T
    product = folded(wide[: 2 * RHS], SHARE)
    low = (wide[2 * RHS : 3 * RHS] + wide[3 * RHS :] * (1.0 / LOW_SCALE)) * (SHARE / REST_SCALE)
    own_ref[...] = (product + low) + folded(total_ref[...], 4.0 * SHARE)


def sums_kernel(
    own_ref, back_ref, other_ref, dir_ref, swap_dir_ref, res_ref, swap_res_ref, product_ref, sums_ref
):
    mine = handles_own_block()
    vecs = jnp.where(mine, dir_ref[...], swap_dir_ref[...])
    res = jnp.where(mine, res_ref[...], swap_res_ref[...])
    product = (own_ref[...] + back_ref[...]) + other_ref[...]
    product_ref[...] = product
    image = product + NOISE * vecs
    lane = lax.broadcasted_iota(jnp.int32, (RHS, 128), 1)
    table = jnp.zeros((RHS, 128), F32)
    for i, (a, b) in enumerate(((res, res), (vecs, image), (res, image), (image, image))):
        table = jnp.where(lane == i, jnp.sum(a * b, 1, keepdims=True), table)
    table = jnp.concatenate([table, jnp.zeros((128 - RHS, 128), F32)], 0).T
    row = jnp.concatenate([table[i : i + 1, :RHS] for i in range(4)], 1)
    sums_ref[...] = jnp.broadcast_to(row[None], sums_ref.shape)


def update_kernel(
    sums_ref, active_ref, image_ref, other_ref, dir_ref, res_ref, sol_ref,
    sol_out, res_out, dir_out, sol_next, res_next, dir_next, sent,
):
    row = jnp.sum(sums_ref[...], 0)
    table = jnp.concatenate([row[:, i * RHS : (i + 1) * RHS] for i in range(4)], 0)
    table = jnp.concatenate([table, jnp.zeros((4, RHS), F32)], 0)
    table = jnp.concatenate([table, jnp.zeros((8, 128 - RHS), F32)], 1)
    table = jnp.concatenate([table, jnp.zeros((120, 128), F32)], 0).T
    norm_old, curvature = table[:RHS, 0:1], table[:RHS, 1:2]
    res_image, image_image = table[:RHS, 2:3], table[:RHS, 3:4]
    active = as_column(active_ref[...])
    alpha = active.astype(F32) * norm_old / curvature
    norm_new = norm_old - 2.0 * alpha * res_image + alpha * alpha * image_image
    ratio = norm_new / norm_old
    mine = handles_own_block()
    copies = []
    for k in range(4):
        rows = slice(k * 8, k * 8 + 8)
        vecs = dir_ref[rows]
        image = jnp.where(mine, image_ref[rows], other_ref[rows]) + NOISE * vecs
        sol_next[rows] = sol_ref[rows] + alpha[rows] * vecs
        after = res_ref[rows] - alpha[rows] * image
        res_next[rows] = after
        dir_next[rows] = jnp.where(active[rows] == 1, after + ratio[rows] * vecs, vecs)
        for n, (source, target) in enumerate(((sol_next, sol_out), (res_next, res_out), (dir_next, dir_out))):
            copies.append(pltpu.make_async_copy(source.at[rows], target.at[rows], sent.at[3 * k + n]))
            copies[-1].start()
    for copy in copies:
        copy.wait()


def permuted(value, change):
    pairs = []
    for index in range(256):
        block, rep = index // 2, index % 2
        to = change(block, block % 2, rep)
        if to is not None:
            pairs.append((index, to[0] % 128 * 2 + to[1]))
    return lax.ppermute(value, AXES, pairs)


def to_partner(block, core, rep):
    if core == rep:
        return block + 32, rep
    return block - 32 - 2 * rep, rep


def to_home(block, core, rep):
    if core == rep:
        return block - 32, rep
    return block + 31 + 4 * rep, 1 - rep


def swap_core(block, core, rep):
    return block ^ 1, rep


def to_twin(block, core, rep):
    return (block, 1 - rep) if core == rep else None


def over_chips(value):
    groups = [[block * 2 + rep for block in range(core, 128, 2) for rep in range(2)] for core in range(2)]
    return lax.all_to_all(value, AXES, 0, 0, axis_index_groups=groups)


def call(kernel, outs, ins, scratch=(), name=None, out_space=pltpu.VMEM):
    vmem = pl.BlockSpec(memory_space=pltpu.VMEM)
    hbm = pl.BlockSpec(memory_space=pltpu.HBM)
    run = pl.pallas_call(
        kernel,
        out_shape=tuple(jax.ShapeDtypeStruct(*(out if isinstance(out[0], tuple) else (out, F32))) for out in outs),
        in_specs=[hbm if i == "h" else vmem for i in ins],
        out_specs=(pl.BlockSpec(memory_space=out_space),) * len(outs),
        scratch_shapes=scratch,
        compiler_params=pltpu.CompilerParams(vmem_limit_bytes=28 * 2**20),
        name=name,
    )

    def placed(*args):
        return run(*(pltpu.with_memory_space_constraint(a, pltpu.HBM) if i == "h" else a for i, a in zip(ins, args)))

    return placed


def on_device(points, inv_length, direction, residual, solution, active):
    lengths = inv_length.reshape(1, DIM)
    far_pts = permuted(points, to_partner)
    swap_pts = permuted(points, swap_core)
    swap_dir = permuted(direction, swap_core)
    swap_res = permuted(residual, swap_core)
    whole = (RHS, BLOCK)
    left_shape, right_shape = ((BLOCK, DEPTH), BF16), ((DEPTH, BLOCK), BF16)
    vecs_shape, total_shape = ((2 * RHS, BLOCK), BF16), ((2 * RHS, BLOCK), F32)
    left, right, vecs, total, scale = call(
        start_kernel,
        [left_shape, right_shape, vecs_shape, total_shape, (DIM, 128)],
        "hvhhv",
        [
            pltpu.VMEM(whole, F32),
            pltpu.VMEM(whole, F32),
            pltpu.VMEM((1, DIM), F32),
            pltpu.SemaphoreType.DMA((9,)),
        ],
        "own_start",
    )(points, swap_pts, lengths, direction, swap_dir)
    later, scale = lax.optimization_barrier((direction, scale))
    far_dir = permuted(later, to_partner)
    total, scale = call(
        early_kernel, [total_shape, (DIM, 128)], "vvvvv", name="own_early"
    )(left, right, vecs, total, scale)
    back, kernel = call(
        kernel_kernel,
        [whole, (BLOCK, BLOCK)],
        "vvvv",
        [
            pltpu.VMEM(*right_shape),
            pltpu.VMEM(*total_shape),
            pltpu.VMEM((2, TILE, WIDTH), F32),
            pltpu.VMEM((2, 2, TILE, WIDTH), BF16),
        ],
        "cross_kernel",
    )(left, vecs, far_pts, scale)
    total, back = call(late_kernel, [total_shape, whole], "vvvvv", name="own_late")(
        left, right, vecs, total, back
    )
    back = permuted(back, to_home)
    tall = (BLOCK, 128)
    (own,) = call(
        product_kernel,
        [whole],
        "vvv",
        [pltpu.VMEM(tall, BF16), pltpu.VMEM(tall, F8), pltpu.VMEM(tall, F32)],
        "cross_product",
    )(kernel, far_dir, total)
    part = own + back
    other = permuted(part, swap_core)
    product, sums = call(sums_kernel, [whole, (128, 1, 128)], "vvvvvvv", name="sums")(
        own, back, other, direction, swap_dir, residual, swap_res
    )
    twin = permuted(product, to_twin)
    return call(
        update_kernel,
        [whole] * 3,
        "vvvvvvv",
        [pltpu.VMEM(whole, F32)] * 3 + [pltpu.SemaphoreType.DMA((12,))],
        "update",
        pltpu.HBM,
    )(
        over_chips(sums), active.reshape(1, RHS), product, twin, direction, residual, solution
    )


def solution(mesh):
    placed = (P(None, "blk"), P(), P(None, "blk"), P(None, "blk"), P(None, "blk"), P())
    return jax.shard_map(
        on_device,
        mesh=mesh,
        in_specs=placed,
        out_specs=(P(None, "blk"), P(None, "blk"), P(None, "blk")),
        check_vma=False,
    )
```

```python
import functools
import math

import jax
import jax.numpy as jnp
from jax import lax
from jax.experimental import pallas as pl
from jax.experimental.pallas import tpu as pltpu
from jax.sharding import PartitionSpec as P

F32, BF16, F8 = jnp.float32, jnp.bfloat16, jnp.float8_e4m3fn
ROOT_FIVE = math.sqrt(5.0)
LOG2_E = 1.4426950408889634
SCALE = ROOT_FIVE * LOG2_E
SHARE = 1.0 / (3.0 * LOG2_E * LOG2_E)
NOISE = 0.5
BLOCK = 2048
DIM = 32
RHS = 32
TILE = 512
STEPS = BLOCK // TILE
WIDTH = 256
ACROSS = BLOCK // WIDTH
REST_SCALE = 2.0**14
LOW_SCALE = 2.0**4
DEPTH = 256
AXES = ("blk", "rep")
NT = (((1,), (1,)), ((), ()))


def pieces(value, count):
    out = []
    for _ in range(count):
        head = value.astype(BF16)
        out.append(head)
        value = value - head.astype(F32)
    return out


def norm_rows(points):
    return [part.astype(F32) for part in pieces(jnp.sum(points * points, 0, keepdims=True), 3)]


def left_side(points):
    n = points.shape[1]
    p = pieces(points, 3)
    m = norm_rows(points)
    row = lax.broadcasted_iota(jnp.int32, (16, n), 0)
    tail = jnp.where(row < 6, 1.0, 0.0)
    for i in range(3):
        tail = jnp.where(row == i, m[i], tail)
    rest = jnp.zeros((DEPTH - 6 * DIM - 16, n), BF16)
    return jnp.concatenate([p[0], p[0], p[1], p[1], p[0], p[2], tail.astype(BF16), rest], 0)


def right_side(points):
    n = points.shape[1]
    p = [(-2.0 * part.astype(F32)).astype(BF16) for part in pieces(points, 3)]
    m = norm_rows(points)
    row = lax.broadcasted_iota(jnp.int32, (16, n), 0)
    tail = jnp.where(row < 3, 1.0, 0.0)
    for i in range(3):
        tail = jnp.where(row == 3 + i, m[i], tail)
    rest = jnp.zeros((DEPTH - 6 * DIM - 16, n), BF16)
    return jnp.concatenate([p[0], p[1], p[0], p[1], p[2], p[0], tail.astype(BF16), rest], 0)


def both_pieces(vectors):
    return jnp.concatenate(pieces(vectors, 2), 0)


def squares(left, right):
    return jnp.maximum(jnp.dot(left, right, preferred_element_type=F32), 1e-30)


def matern(sq):
    dist = sq * lax.rsqrt(sq)
    return (dist * (dist + 3.0 * LOG2_E) + 3.0 * LOG2_E * LOG2_E) * jnp.exp2(-dist)


def halves(kernel):
    head = kernel.astype(BF16)
    return head, (kernel - head.astype(F32)).astype(BF16)


def add_rows(total, rows, vecs, cols, kernel):
    head, rest = kernel
    total[:, rows] += lax.dot_general(vecs[:, cols], head, NT, preferred_element_type=F32)
    total[:RHS, rows] += lax.dot_general(vecs[:RHS, cols], rest, NT, preferred_element_type=F32)


def add_columns(total, cols, vecs, rows, kernel):
    head, rest = kernel
    total[:, cols] += jnp.dot(vecs[:, rows], head, preferred_element_type=F32)
    total[:RHS, cols] += jnp.dot(vecs[:RHS, rows], rest, preferred_element_type=F32)


def span(index):
    return pl.ds(pl.multiple_of(index * TILE, TILE), TILE)


def as_column(row):
    n = row.shape[1]
    square = lax.broadcasted_iota(jnp.int32, (n, n), 0) == lax.broadcasted_iota(jnp.int32, (n, n), 1)
    return jnp.sum(jnp.where(square, row, jnp.zeros_like(row)), 1, keepdims=True)


def folded(total, scale):
    return (total[:RHS] + total[RHS:]) * scale


def handles_own_block():
    return lax.rem(lax.axis_index("blk"), 2) == lax.axis_index("rep")


def waits_longest():
    return jnp.logical_and(lax.rem(lax.axis_index("blk"), 4) == 2, lax.axis_index("rep") == 1)


def own_tiles(left, right, vecs, total, first):
    half = lax.rem(lax.axis_index("blk"), 2)

    def diagonal(i):
        rows = span(i)
        add_columns(total, rows, vecs, rows, halves(matern(squares(left[rows, :], right[:, rows]))))

    def pair(i, j):
        rows, cols = span(i), span(j)
        kernel = halves(matern(squares(left[rows, :], right[:, cols])))
        add_rows(total, rows, vecs, cols, kernel)
        add_columns(total, cols, vecs, rows, kernel)

    i = half * (STEPS // 2)
    if first:
        diagonal(i)
        pair(i, i + 1)
    else:
        diagonal(i + 1)
        pair(i + 1, lax.rem(i + 2, STEPS))
        pair(half, half + STEPS // 2)


def start_kernel(
    pts_ref, swap_pts_ref, len_ref, dir_ref, swap_dir_ref,
    left, right, vecs, total, scale_ref, pts, dirs, lengths, arrived,
):
    copies = [pltpu.make_async_copy(len_ref, lengths, arrived.at[8])]
    for n, (source, target) in enumerate(((pts_ref, pts), (dir_ref, dirs))):
        for k in range(4):
            rows = slice(k * 8, k * 8 + 8)
            copies.append(pltpu.make_async_copy(source.at[rows], target.at[rows], arrived.at[4 * n + k]))
    for copy in copies:
        copy.start()
    mine = handles_own_block()
    total[...] = jnp.zeros_like(total)
    for copy in copies:
        copy.wait()
    scale = as_column(lengths[...]) * SCALE
    scale_ref[...] = jnp.broadcast_to(scale, scale_ref.shape)
    points = jnp.where(mine, pts[...], swap_pts_ref[...]) * scale
    left[...] = left_side(points).T
    right[...] = right_side(points)
    vecs[...] = both_pieces(jnp.where(mine, dirs[...], swap_dir_ref[...]))
    own_tiles(left, right, vecs, total, True)


def early_kernel(left, right, vecs, total_in, scale_in, total, scale):
    total[...] = total_in[...]
    scale[...] = scale_in[...]

    @pl.when(waits_longest())
    def _():
        own_tiles(left, right, vecs, total, False)


def late_kernel(left, right, vecs, total_in, back_in, total, back):
    total[...] = total_in[...]
    back[...] = back_in[...]

    @pl.when(jnp.logical_not(waits_longest()))
    def _():
        own_tiles(left, right, vecs, total, False)


def kernel_kernel(left, vecs, far_pts_ref, scale_ref, back_ref, kernel_ref, right, total, sq, parts):
    right[...] = right_side(far_pts_ref[...] * scale_ref[:, 0:1])
    total[...] = jnp.zeros_like(total)
    cols = [slice(c * WIDTH, (c + 1) * WIDTH) for c in range(ACROSS)]

    def distances(r, c):
        sq[c % 2] = squares(left[span(r), :], right[:, cols[c]])

    def product(r, c):
        add_columns(total, cols[c], vecs, span(r), (parts[c % 2, 0], parts[c % 2, 1]))

    distances(0, 0)

    def some_rows(r, carry):
        for c in range(ACROSS):
            if c + 1 < ACROSS:
                distances(r, c + 1)
            else:
                distances(jnp.minimum(r + 1, STEPS - 1), 0)
            kernel = matern(sq[c % 2])
            kernel_ref[span(r), cols[c]] = kernel
            parts[c % 2, 0], parts[c % 2, 1] = halves(kernel)
            if c > 0:
                product(r, c - 1)
        product(r, ACROSS - 1)
        return carry

    lax.fori_loop(0, STEPS, some_rows, 0)
    back_ref[...] = folded(total[...], SHARE)


def product_kernel(kernel_ref, far_dir_ref, total_ref, own_ref, far_vecs, far_coarse, tall):
    vecs = far_dir_ref[...]
    coarse = vecs.astype(F8).astype(F32)
    fine = ((vecs - coarse) * LOW_SCALE).astype(F8).astype(F32)
    columns = jnp.concatenate([part.astype(F32) for part in pieces(vecs, 2)] + [coarse, fine], 0).T
    far_vecs[...] = columns.astype(BF16)
    far_coarse[...] = columns.astype(F8)
    from_head = lax.broadcasted_iota(jnp.int32, (TILE, 128), 1) < 2 * RHS

    def some_rows(r, carry):
        kernel = kernel_ref[span(r), :]
        head = kernel.astype(BF16)
        rest = ((kernel - head.astype(F32)) * REST_SCALE).astype(F8)
        tall[span(r), :] = jnp.where(
            from_head,
            jnp.dot(head, far_vecs[...], preferred_element_type=F32),
            jnp.dot(rest, far_coarse[...], preferred_element_type=F32),
        )
        return carry

    lax.fori_loop(0, STEPS, some_rows, 0)
    wide = tall[...].T
    product = folded(wide[: 2 * RHS], SHARE)
    low = (wide[2 * RHS : 3 * RHS] + wide[3 * RHS :] * (1.0 / LOW_SCALE)) * (SHARE / REST_SCALE)
    own_ref[...] = (product + low) + folded(total_ref[...], 4.0 * SHARE)


def sums_kernel(
    part_ref, other_ref, dir_ref, swap_dir_ref, res_ref, swap_res_ref, product_ref, sums_ref
):
    mine = handles_own_block()
    vecs = jnp.where(mine, dir_ref[...], swap_dir_ref[...])
    res = jnp.where(mine, res_ref[...], swap_res_ref[...])
    product = part_ref[...] + other_ref[...]
    product_ref[...] = product
    image = product + NOISE * vecs
    lane = lax.broadcasted_iota(jnp.int32, (RHS, 128), 1)
    table = jnp.zeros((RHS, 128), F32)
    for i, (a, b) in enumerate(((res, res), (vecs, image), (res, image), (image, image))):
        table = jnp.where(lane == i, jnp.sum(a * b, 1, keepdims=True), table)
    table = jnp.concatenate([table, jnp.zeros((128 - RHS, 128), F32)], 0).T
    row = jnp.concatenate([table[i : i + 1, :RHS] for i in range(4)], 1)
    sums_ref[...] = jnp.broadcast_to(row[None], sums_ref.shape)


def update_kernel(
    sums_ref, active_ref, image_ref, other_ref, dir_ref, res_ref, sol_ref,
    sol_out, res_out, dir_out, sol_next, res_next, dir_next, sent,
):
    row = jnp.sum(sums_ref[...], 0)
    table = jnp.concatenate([row[:, i * RHS : (i + 1) * RHS] for i in range(4)], 0)
    table = jnp.concatenate([table, jnp.zeros((4, RHS), F32)], 0)
    table = jnp.concatenate([table, jnp.zeros((8, 128 - RHS), F32)], 1)
    table = jnp.concatenate([table, jnp.zeros((120, 128), F32)], 0).T
    norm_old, curvature = table[:RHS, 0:1], table[:RHS, 1:2]
    res_image, image_image = table[:RHS, 2:3], table[:RHS, 3:4]
    active = as_column(active_ref[...])
    alpha = active.astype(F32) * norm_old / curvature
    norm_new = norm_old - 2.0 * alpha * res_image + alpha * alpha * image_image
    ratio = norm_new / norm_old
    mine = handles_own_block()
    copies = []
    for k in range(4):
        rows = slice(k * 8, k * 8 + 8)
        vecs = dir_ref[rows]
        image = jnp.where(mine, image_ref[rows], other_ref[rows]) + NOISE * vecs
        sol_next[rows] = sol_ref[rows] + alpha[rows] * vecs
        after = res_ref[rows] - alpha[rows] * image
        res_next[rows] = after
        dir_next[rows] = jnp.where(active[rows] == 1, after + ratio[rows] * vecs, vecs)
        for n, (source, target) in enumerate(((sol_next, sol_out), (res_next, res_out), (dir_next, dir_out))):
            copies.append(pltpu.make_async_copy(source.at[rows], target.at[rows], sent.at[3 * k + n]))
            copies[-1].start()
    for copy in copies:
        copy.wait()


def permuted(value, change):
    pairs = []
    for index in range(256):
        block, rep = index // 2, index % 2
        to = change(block, block % 2, rep)
        pairs.append((index, to[0] % 128 * 2 + to[1]))
    return lax.ppermute(value, AXES, pairs)


def to_partner(block, core, rep):
    if core == rep:
        to = (block + 32, rep)
    else:
        to = (block - 32 - 2 * rep, rep)
    if block % 32 == 0:
        to = (block - 34, 1) if rep == 0 else (block + 32, 0)
    return to


def to_home(block, core, rep):
    if core == rep:
        return block - 32, rep
    return block + 31 + 4 * rep, 1 - rep


def swap_core(block, core, rep):
    return block ^ 1, rep


def swap_rep(block, core, rep):
    return block, 1 - rep


def over_chips(value):
    groups = [[block * 2 + rep for block in range(core, 128, 2) for rep in range(2)] for core in range(2)]
    return lax.all_to_all(value, AXES, 0, 0, axis_index_groups=groups)


def call(kernel, outs, ins, scratch=(), name=None, out_space=pltpu.VMEM):
    vmem = pl.BlockSpec(memory_space=pltpu.VMEM)
    hbm = pl.BlockSpec(memory_space=pltpu.HBM)
    run = pl.pallas_call(
        kernel,
        out_shape=tuple(jax.ShapeDtypeStruct(*(out if isinstance(out[0], tuple) else (out, F32))) for out in outs),
        in_specs=[hbm if i == "h" else vmem for i in ins],
        out_specs=(pl.BlockSpec(memory_space=out_space),) * len(outs),
        scratch_shapes=scratch,
        compiler_params=pltpu.CompilerParams(vmem_limit_bytes=28 * 2**20),
        name=name,
    )

    def placed(*args):
        return run(*(pltpu.with_memory_space_constraint(a, pltpu.HBM) if i == "h" else a for i, a in zip(ins, args)))

    return placed


def on_device(points, inv_length, direction, residual, solution, active):
    lengths = inv_length.reshape(1, DIM)
    far_pts = permuted(points, to_partner)
    swap_pts = permuted(points, swap_core)
    swap_dir = permuted(direction, swap_core)
    swap_res = permuted(residual, swap_core)
    whole = (RHS, BLOCK)
    left_shape, right_shape = ((BLOCK, DEPTH), BF16), ((DEPTH, BLOCK), BF16)
    vecs_shape, total_shape = ((2 * RHS, BLOCK), BF16), ((2 * RHS, BLOCK), F32)
    left, right, vecs, total, scale = call(
        start_kernel,
        [left_shape, right_shape, vecs_shape, total_shape, (DIM, 128)],
        "hvhhv",
        [
            pltpu.VMEM(whole, F32),
            pltpu.VMEM(whole, F32),
            pltpu.VMEM((1, DIM), F32),
            pltpu.SemaphoreType.DMA((9,)),
        ],
        "own_start",
    )(points, swap_pts, lengths, direction, swap_dir)
    later, scale = lax.optimization_barrier((direction, scale))
    far_dir = permuted(later, to_partner)
    total, scale = call(
        early_kernel, [total_shape, (DIM, 128)], "vvvvv", name="own_early"
    )(left, right, vecs, total, scale)
    back, kernel = call(
        kernel_kernel,
        [whole, (BLOCK, BLOCK)],
        "vvvv",
        [
            pltpu.VMEM(*right_shape),
            pltpu.VMEM(*total_shape),
            pltpu.VMEM((2, TILE, WIDTH), F32),
            pltpu.VMEM((2, 2, TILE, WIDTH), BF16),
        ],
        "cross_kernel",
    )(left, vecs, far_pts, scale)
    total, back = call(late_kernel, [total_shape, whole], "vvvvv", name="own_late")(
        left, right, vecs, total, back
    )
    back = permuted(back, to_home)
    tall = (BLOCK, 128)
    (own,) = call(
        product_kernel,
        [whole],
        "vvv",
        [pltpu.VMEM(tall, BF16), pltpu.VMEM(tall, F8), pltpu.VMEM(tall, F32)],
        "cross_product",
    )(kernel, far_dir, total)
    part = own + back
    other = permuted(part, swap_core)
    product, sums = call(sums_kernel, [whole, (128, 1, 128)], "vvvvvv", name="sums")(
        part, other, direction, swap_dir, residual, swap_res
    )
    twin = permuted(product, swap_rep)
    return call(
        update_kernel,
        [whole] * 3,
        "vvvvvvv",
        [pltpu.VMEM(whole, F32)] * 3 + [pltpu.SemaphoreType.DMA((12,))],
        "update",
        pltpu.HBM,
    )(
        over_chips(sums), active.reshape(1, RHS), product, twin, direction, residual, solution
    )


def solution(mesh):
    placed = (P(None, "blk"), P(), P(None, "blk"), P(None, "blk"), P(None, "blk"), P())
    return jax.shard_map(
        on_device,
        mesh=mesh,
        in_specs=placed,
        out_specs=(P(None, "blk"), P(None, "blk"), P(None, "blk")),
        check_vma=False,
    )
```

```python
import functools
import math

import jax
import jax.numpy as jnp
from jax import lax
from jax.experimental import pallas as pl
from jax.experimental.pallas import tpu as pltpu
from jax.sharding import PartitionSpec as P

F32, BF16, F8 = jnp.float32, jnp.bfloat16, jnp.float8_e4m3fn
ROOT_FIVE = math.sqrt(5.0)
LOG2_E = 1.4426950408889634
SCALE = ROOT_FIVE * LOG2_E
SHARE = 1.0 / (3.0 * LOG2_E * LOG2_E)
NOISE = 0.5
BLOCK = 2048
DIM = 32
RHS = 32
TILE = 512
STEPS = BLOCK // TILE
WIDTH = 256
ACROSS = BLOCK // WIDTH
REST_SCALE = 2.0**14
LOW_SCALE = 2.0**4
DEPTH = 256
AXES = ("blk", "rep")
NT = (((1,), (1,)), ((), ()))


def pieces(value, count):
    out = []
    for _ in range(count):
        head = value.astype(BF16)
        out.append(head)
        value = value - head.astype(F32)
    return out


def norm_rows(points):
    return [part.astype(F32) for part in pieces(jnp.sum(points * points, 0, keepdims=True), 3)]


def left_side(points):
    n = points.shape[1]
    p = pieces(points, 3)
    m = norm_rows(points)
    row = lax.broadcasted_iota(jnp.int32, (16, n), 0)
    tail = jnp.where(row < 6, 1.0, 0.0)
    for i in range(3):
        tail = jnp.where(row == i, m[i], tail)
    rest = jnp.zeros((DEPTH - 6 * DIM - 16, n), BF16)
    return jnp.concatenate([p[0], p[0], p[1], p[1], p[0], p[2], tail.astype(BF16), rest], 0)


def right_side(points):
    n = points.shape[1]
    p = [(-2.0 * part.astype(F32)).astype(BF16) for part in pieces(points, 3)]
    m = norm_rows(points)
    row = lax.broadcasted_iota(jnp.int32, (16, n), 0)
    tail = jnp.where(row < 3, 1.0, 0.0)
    for i in range(3):
        tail = jnp.where(row == 3 + i, m[i], tail)
    rest = jnp.zeros((DEPTH - 6 * DIM - 16, n), BF16)
    return jnp.concatenate([p[0], p[1], p[0], p[1], p[2], p[0], tail.astype(BF16), rest], 0)


def both_pieces(vectors):
    return jnp.concatenate(pieces(vectors, 2), 0)


def squares(left, right):
    return jnp.maximum(jnp.dot(left, right, preferred_element_type=F32), 1e-30)


def matern(sq):
    dist = sq * lax.rsqrt(sq)
    return (dist * (dist + 3.0 * LOG2_E) + 3.0 * LOG2_E * LOG2_E) * jnp.exp2(-dist)


def halves(kernel):
    head = kernel.astype(BF16)
    return head, (kernel - head.astype(F32)).astype(BF16)


def add_rows(total, rows, vecs, cols, kernel):
    head, rest = kernel
    total[:, rows] += lax.dot_general(vecs[:, cols], head, NT, preferred_element_type=F32)
    total[:RHS, rows] += lax.dot_general(vecs[:RHS, cols], rest, NT, preferred_element_type=F32)


def add_columns(total, cols, vecs, rows, kernel):
    head, rest = kernel
    total[:, cols] += jnp.dot(vecs[:, rows], head, preferred_element_type=F32)
    total[:RHS, cols] += jnp.dot(vecs[:RHS, rows], rest, preferred_element_type=F32)


def span(index):
    return pl.ds(pl.multiple_of(index * TILE, TILE), TILE)


def as_column(row):
    n = row.shape[1]
    square = lax.broadcasted_iota(jnp.int32, (n, n), 0) == lax.broadcasted_iota(jnp.int32, (n, n), 1)
    return jnp.sum(jnp.where(square, row, jnp.zeros_like(row)), 1, keepdims=True)


def folded(total, scale):
    return (total[:RHS] + total[RHS:]) * scale


def handles_own_block():
    return lax.rem(lax.axis_index("blk"), 2) == lax.axis_index("rep")


def waits_longest():
    return jnp.logical_and(lax.rem(lax.axis_index("blk"), 4) == 2, lax.axis_index("rep") == 1)


def own_tiles(left, right, vecs, total, first):
    half = lax.rem(lax.axis_index("blk"), 2)

    def diagonal(i):
        rows = span(i)
        add_columns(total, rows, vecs, rows, halves(matern(squares(left[rows, :], right[:, rows]))))

    def pair(i, j):
        rows, cols = span(i), span(j)
        kernel = halves(matern(squares(left[rows, :], right[:, cols])))
        add_rows(total, rows, vecs, cols, kernel)
        add_columns(total, cols, vecs, rows, kernel)

    i = half * (STEPS // 2)
    if first:
        diagonal(i)
        pair(i, i + 1)
    else:
        diagonal(i + 1)
        pair(i + 1, lax.rem(i + 2, STEPS))
        pair(half, half + STEPS // 2)


def start_kernel(
    pts_ref, swap_pts_ref, len_ref, dir_ref, swap_dir_ref,
    left, right, vecs, total, scale_ref, pts, dirs, lengths, arrived,
):
    copies = [pltpu.make_async_copy(len_ref, lengths, arrived.at[8])]
    for n, (source, target) in enumerate(((pts_ref, pts), (dir_ref, dirs))):
        for k in range(4):
            rows = slice(k * 8, k * 8 + 8)
            copies.append(pltpu.make_async_copy(source.at[rows], target.at[rows], arrived.at[4 * n + k]))
    for copy in copies:
        copy.start()
    mine = handles_own_block()
    total[...] = jnp.zeros_like(total)
    for copy in copies:
        copy.wait()
    scale = as_column(lengths[...]) * SCALE
    scale_ref[...] = jnp.broadcast_to(scale, scale_ref.shape)
    points = jnp.where(mine, pts[...], swap_pts_ref[...]) * scale
    left[...] = left_side(points).T
    right[...] = right_side(points)
    vecs[...] = both_pieces(jnp.where(mine, dirs[...], swap_dir_ref[...]))
    own_tiles(left, right, vecs, total, True)


def early_kernel(left, right, vecs, total_in, scale_in, total, scale):
    total[...] = total_in[...]
    scale[...] = scale_in[...]

    @pl.when(waits_longest())
    def _():
        own_tiles(left, right, vecs, total, False)


def late_kernel(left, right, vecs, total_in, back_in, total, back):
    total[...] = total_in[...]
    back[...] = back_in[...]

    @pl.when(jnp.logical_not(waits_longest()))
    def _():
        own_tiles(left, right, vecs, total, False)


def kernel_kernel(left, vecs, far_pts_ref, scale_ref, back_ref, kernel_ref, right, total, sq, parts):
    right[...] = right_side(far_pts_ref[...] * scale_ref[:, 0:1])
    total[...] = jnp.zeros_like(total)
    cols = [slice(c * WIDTH, (c + 1) * WIDTH) for c in range(ACROSS)]

    def distances(r, c):
        sq[c % 2] = squares(left[span(r), :], right[:, cols[c]])

    def product(r, c):
        add_columns(total, cols[c], vecs, span(r), (parts[c % 2, 0], parts[c % 2, 1]))

    distances(0, 0)

    def some_rows(r, carry):
        for c in range(ACROSS):
            if c + 1 < ACROSS:
                distances(r, c + 1)
            else:
                distances(jnp.minimum(r + 1, STEPS - 1), 0)
            kernel = matern(sq[c % 2])
            kernel_ref[span(r), cols[c]] = kernel
            parts[c % 2, 0], parts[c % 2, 1] = halves(kernel)
            if c > 0:
                product(r, c - 1)
        product(r, ACROSS - 1)
        return carry

    lax.fori_loop(0, STEPS, some_rows, 0)
    back_ref[...] = folded(total[...], SHARE)


def product_kernel(kernel_ref, far_dir_ref, total_ref, own_ref, far_vecs, far_coarse, tall):
    vecs = far_dir_ref[...]
    coarse = vecs.astype(F8).astype(F32)
    fine = ((vecs - coarse) * LOW_SCALE).astype(F8).astype(F32)
    columns = jnp.concatenate([part.astype(F32) for part in pieces(vecs, 2)] + [coarse, fine], 0).T
    far_vecs[...] = columns.astype(BF16)
    far_coarse[...] = columns.astype(F8)
    from_head = lax.broadcasted_iota(jnp.int32, (TILE, 128), 1) < 2 * RHS

    def some_rows(r, carry):
        kernel = kernel_ref[span(r), :]
        head = kernel.astype(BF16)
        rest = ((kernel - head.astype(F32)) * REST_SCALE).astype(F8)
        tall[span(r), :] = jnp.where(
            from_head,
            jnp.dot(head, far_vecs[...], preferred_element_type=F32),
            jnp.dot(rest, far_coarse[...], preferred_element_type=F32),
        )
        return carry

    lax.fori_loop(0, STEPS, some_rows, 0)
    wide = tall[...].T
    product = folded(wide[: 2 * RHS], SHARE)
    low = (wide[2 * RHS : 3 * RHS] + wide[3 * RHS :] * (1.0 / LOW_SCALE)) * (SHARE / REST_SCALE)
    own_ref[...] = (product + low) + folded(total_ref[...], 4.0 * SHARE)


def sums_kernel(
    part_ref, other_ref, dir_ref, swap_dir_ref, res_ref, swap_res_ref, product_ref, sums_ref
):
    mine = handles_own_block()
    vecs = jnp.where(mine, dir_ref[...], swap_dir_ref[...])
    res = jnp.where(mine, res_ref[...], swap_res_ref[...])
    product = part_ref[...] + other_ref[...]
    product_ref[...] = product
    image = product + NOISE * vecs
    lane = lax.broadcasted_iota(jnp.int32, (RHS, 128), 1)
    table = jnp.zeros((RHS, 128), F32)
    for i, (a, b) in enumerate(((res, res), (vecs, image), (res, image), (image, image))):
        table = jnp.where(lane == i, jnp.sum(a * b, 1, keepdims=True), table)
    table = jnp.concatenate([table, jnp.zeros((128 - RHS, 128), F32)], 0).T
    row = jnp.concatenate([table[i : i + 1, :RHS] for i in range(4)], 1)
    sums_ref[...] = jnp.broadcast_to(row[None], sums_ref.shape)


def update_kernel(
    sums_ref, active_ref, image_ref, other_ref, dir_ref, res_ref, sol_ref,
    sol_out, res_out, dir_out, sol_next, res_next, dir_next, sent,
):
    row = jnp.sum(sums_ref[...], 0)
    table = jnp.concatenate([row[:, i * RHS : (i + 1) * RHS] for i in range(4)], 0)
    table = jnp.concatenate([table, jnp.zeros((4, RHS), F32)], 0)
    table = jnp.concatenate([table, jnp.zeros((8, 128 - RHS), F32)], 1)
    table = jnp.concatenate([table, jnp.zeros((120, 128), F32)], 0).T
    norm_old, curvature = table[:RHS, 0:1], table[:RHS, 1:2]
    res_image, image_image = table[:RHS, 2:3], table[:RHS, 3:4]
    active = as_column(active_ref[...])
    alpha = active.astype(F32) * norm_old / curvature
    norm_new = norm_old - 2.0 * alpha * res_image + alpha * alpha * image_image
    ratio = norm_new / norm_old
    mine = handles_own_block()
    copies = []
    for k in range(4):
        rows = slice(k * 8, k * 8 + 8)
        vecs = dir_ref[rows]
        image = jnp.where(mine, image_ref[rows], other_ref[rows]) + NOISE * vecs
        sol_next[rows] = sol_ref[rows] + alpha[rows] * vecs
        after = res_ref[rows] - alpha[rows] * image
        res_next[rows] = after
        dir_next[rows] = jnp.where(active[rows] == 1, after + ratio[rows] * vecs, vecs)
        for n, (source, target) in enumerate(((sol_next, sol_out), (res_next, res_out), (dir_next, dir_out))):
            copies.append(pltpu.make_async_copy(source.at[rows], target.at[rows], sent.at[3 * k + n]))
            copies[-1].start()
    for copy in copies:
        copy.wait()


def permuted(value, change):
    pairs = []
    for index in range(256):
        block, rep = index // 2, index % 2
        to = change(block, block % 2, rep)
        pairs.append((index, to[0] % 128 * 2 + to[1]))
    return lax.ppermute(value, AXES, pairs)


def to_partner(block, core, rep):
    if core == rep:
        to = (block + 32, rep)
    else:
        to = (block - 32 - 2 * rep, rep)
    if block % 32 == 0:
        to = (block - 34, 1) if rep == 0 else (block + 32, 0)
    return to


def to_home(block, core, rep):
    if core == rep:
        return block - 32, rep
    return block + 31 + 4 * rep, 1 - rep


def swap_core(block, core, rep):
    return block ^ 1, rep


def swap_rep(block, core, rep):
    return block, 1 - rep


def over_chips(value):
    def hops(k):
        x, z, y = k % 4, k // 4 % 8, k // 32
        return -(min(x, 4 - x) + min(y, 4 - y) + min(z, 8 - z)), -k

    groups = [[k // 2 * 4 + core * 2 + k % 2 for k in sorted(range(128), key=hops)] for core in range(2)]
    return lax.all_to_all(value, AXES, 0, 0, axis_index_groups=groups)


def call(kernel, outs, ins, scratch=(), name=None, out_space=pltpu.VMEM):
    vmem = pl.BlockSpec(memory_space=pltpu.VMEM)
    hbm = pl.BlockSpec(memory_space=pltpu.HBM)
    run = pl.pallas_call(
        kernel,
        out_shape=tuple(jax.ShapeDtypeStruct(*(out if isinstance(out[0], tuple) else (out, F32))) for out in outs),
        in_specs=[hbm if i == "h" else vmem for i in ins],
        out_specs=(pl.BlockSpec(memory_space=out_space),) * len(outs),
        scratch_shapes=scratch,
        compiler_params=pltpu.CompilerParams(vmem_limit_bytes=28 * 2**20),
        name=name,
    )

    def placed(*args):
        return run(*(pltpu.with_memory_space_constraint(a, pltpu.HBM) if i == "h" else a for i, a in zip(ins, args)))

    return placed


def on_device(points, inv_length, direction, residual, solution, active):
    lengths = inv_length.reshape(1, DIM)
    far_pts = permuted(points, to_partner)
    swap_pts = permuted(points, swap_core)
    swap_dir = permuted(direction, swap_core)
    swap_res = permuted(residual, swap_core)
    whole = (RHS, BLOCK)
    left_shape, right_shape = ((BLOCK, DEPTH), BF16), ((DEPTH, BLOCK), BF16)
    vecs_shape, total_shape = ((2 * RHS, BLOCK), BF16), ((2 * RHS, BLOCK), F32)
    left, right, vecs, total, scale = call(
        start_kernel,
        [left_shape, right_shape, vecs_shape, total_shape, (DIM, 128)],
        "hvhhv",
        [
            pltpu.VMEM(whole, F32),
            pltpu.VMEM(whole, F32),
            pltpu.VMEM((1, DIM), F32),
            pltpu.SemaphoreType.DMA((9,)),
        ],
        "own_start",
    )(points, swap_pts, lengths, direction, swap_dir)
    later, scale = lax.optimization_barrier((direction, scale))
    far_dir = permuted(later, to_partner)
    total, scale = call(
        early_kernel, [total_shape, (DIM, 128)], "vvvvv", name="own_early"
    )(left, right, vecs, total, scale)
    back, kernel = call(
        kernel_kernel,
        [whole, (BLOCK, BLOCK)],
        "vvvv",
        [
            pltpu.VMEM(*right_shape),
            pltpu.VMEM(*total_shape),
            pltpu.VMEM((2, TILE, WIDTH), F32),
            pltpu.VMEM((2, 2, TILE, WIDTH), BF16),
        ],
        "cross_kernel",
    )(left, vecs, far_pts, scale)
    total, back = call(late_kernel, [total_shape, whole], "vvvvv", name="own_late")(
        left, right, vecs, total, back
    )
    back = permuted(back, to_home)
    tall = (BLOCK, 128)
    (own,) = call(
        product_kernel,
        [whole],
        "vvv",
        [pltpu.VMEM(tall, BF16), pltpu.VMEM(tall, F8), pltpu.VMEM(tall, F32)],
        "cross_product",
    )(kernel, far_dir, total)
    part = own + back
    other = permuted(part, swap_core)
    product, sums = call(sums_kernel, [whole, (128, 1, 128)], "vvvvvv", name="sums")(
        part, other, direction, swap_dir, residual, swap_res
    )
    twin = permuted(product, swap_rep)
    return call(
        update_kernel,
        [whole] * 3,
        "vvvvvvv",
        [pltpu.VMEM(whole, F32)] * 3 + [pltpu.SemaphoreType.DMA((12,))],
        "update",
        pltpu.HBM,
    )(
        over_chips(sums), active.reshape(1, RHS), product, twin, direction, residual, solution
    )


def solution(mesh):
    placed = (P(None, "blk"), P(), P(None, "blk"), P(None, "blk"), P(None, "blk"), P())
    return jax.shard_map(
        on_device,
        mesh=mesh,
        in_specs=placed,
        out_specs=(P(None, "blk"), P(None, "blk"), P(None, "blk")),
        check_vma=False,
    )
```

```python
import functools
import math

import jax
import jax.numpy as jnp
from jax import lax
from jax.experimental import pallas as pl
from jax.experimental.pallas import tpu as pltpu
from jax.sharding import PartitionSpec as P

F32, BF16, F8 = jnp.float32, jnp.bfloat16, jnp.float8_e4m3fn
ROOT_FIVE = math.sqrt(5.0)
LOG2_E = 1.4426950408889634
SCALE = ROOT_FIVE * LOG2_E
SHARE = 1.0 / (3.0 * LOG2_E * LOG2_E)
NOISE = 0.5
BLOCK = 2048
DIM = 32
RHS = 32
TILE = 512
STEPS = BLOCK // TILE
WIDTH = 256
HEIGHT = 1024
ACROSS = BLOCK // WIDTH
REST_SCALE = 2.0**14
LOW_SCALE = 2.0**4
DEPTH = 256
AXES = ("blk", "rep")
NT = (((1,), (1,)), ((), ()))


def pieces(value, count):
    out = []
    for _ in range(count):
        head = value.astype(BF16)
        out.append(head)
        value = value - head.astype(F32)
    return out


def norm_rows(points):
    return [part.astype(F32) for part in pieces(jnp.sum(points * points, 0, keepdims=True), 3)]


def left_side(points):
    n = points.shape[1]
    p = [(-2.0 * part.astype(F32)).astype(BF16) for part in pieces(points, 3)]
    m = norm_rows(points)
    row = lax.broadcasted_iota(jnp.int32, (16, n), 0)
    tail = jnp.where(row < 6, 1.0, 0.0)
    for i in range(3):
        tail = jnp.where(row == i, m[i], tail)
    rest = jnp.zeros((DEPTH - 6 * DIM - 16, n), BF16)
    return jnp.concatenate([p[0], p[0], p[1], p[1], p[0], p[2], tail.astype(BF16), rest], 0)


def right_side(points):
    n = points.shape[1]
    p = pieces(points, 3)
    m = norm_rows(points)
    row = lax.broadcasted_iota(jnp.int32, (16, n), 0)
    tail = jnp.where(row < 3, 1.0, 0.0)
    for i in range(3):
        tail = jnp.where(row == 3 + i, m[i], tail)
    rest = jnp.zeros((DEPTH - 6 * DIM - 16, n), BF16)
    return jnp.concatenate([p[0], p[1], p[0], p[1], p[2], p[0], tail.astype(BF16), rest], 0)


def both_pieces(vectors):
    return jnp.concatenate(pieces(vectors, 2), 0)


def squares(left, right):
    return jnp.maximum(jnp.dot(left, right, preferred_element_type=F32), 1e-30)


def matern(sq):
    dist = sq * lax.rsqrt(sq)
    return (dist * (dist + 3.0 * LOG2_E) + 3.0 * LOG2_E * LOG2_E) * jnp.exp2(-dist)


def halves(kernel):
    head = kernel.astype(BF16)
    return head, (kernel - head.astype(F32)).astype(BF16)


def add_rows(total, rows, vecs, cols, kernel):
    head, rest = kernel
    total[:, rows] += lax.dot_general(vecs[:, cols], head, NT, preferred_element_type=F32)
    total[:RHS, rows] += lax.dot_general(vecs[:RHS, cols], rest, NT, preferred_element_type=F32)


def add_columns(total, cols, vecs, rows, kernel):
    head, rest = kernel
    total[:, cols] += jnp.dot(vecs[:, rows], head, preferred_element_type=F32)
    total[:RHS, cols] += jnp.dot(vecs[:RHS, rows], rest, preferred_element_type=F32)


def span(index):
    return pl.ds(pl.multiple_of(index * TILE, TILE), TILE)


def tall_span(index):
    return pl.ds(pl.multiple_of(index * HEIGHT, HEIGHT), HEIGHT)


def as_column(row):
    n = row.shape[1]
    square = lax.broadcasted_iota(jnp.int32, (n, n), 0) == lax.broadcasted_iota(jnp.int32, (n, n), 1)
    return jnp.sum(jnp.where(square, row, jnp.zeros_like(row)), 1, keepdims=True)


def folded(total, scale):
    return (total[:RHS] + total[RHS:]) * scale


def handles_own_block():
    return lax.rem(lax.axis_index("blk"), 2) == lax.axis_index("rep")


def this_core():
    return lax.rem(lax.axis_index("blk"), 2)


def far_from_other_z():
    return jnp.logical_and(lax.rem(lax.axis_index("blk"), 4) >= 2, lax.axis_index("rep") == 1)


def own_tiles(left, right, vecs, total, half, first):
    def diagonal(i):
        rows = span(i)
        add_columns(total, rows, vecs, rows, halves(matern(squares(left[rows, :], right[:, rows]))))

    def pair(i, j):
        rows, cols = span(i), span(j)
        kernel = halves(matern(squares(left[rows, :], right[:, cols])))
        add_rows(total, rows, vecs, cols, kernel)
        add_columns(total, cols, vecs, rows, kernel)

    i = half * (STEPS // 2)
    if first:
        diagonal(i)
        pair(i, i + 1)
    else:
        diagonal(i + 1)
        pair(i + 1, lax.rem(i + 2, STEPS))
        pair(half, half + STEPS // 2)


def start_kernel(
    pts_ref, swap_pts_ref, len_ref, dir_ref, swap_dir_ref,
    left, right, vecs, total, scale_ref, pts, dirs, lengths, arrived,
):
    copies = [pltpu.make_async_copy(len_ref, lengths, arrived.at[8])]
    for n, (source, target) in enumerate(((pts_ref, pts), (dir_ref, dirs))):
        for k in range(4):
            rows = slice(k * 8, k * 8 + 8)
            copies.append(pltpu.make_async_copy(source.at[rows], target.at[rows], arrived.at[4 * n + k]))
    for copy in copies:
        copy.start()
    mine = handles_own_block()
    total[...] = jnp.zeros_like(total)
    for copy in copies:
        copy.wait()
    scale = as_column(lengths[...]) * SCALE
    scale_ref[...] = jnp.broadcast_to(scale, scale_ref.shape)
    points = jnp.where(mine, pts[...], swap_pts_ref[...]) * scale
    left[...] = left_side(points).T
    right[...] = right_side(points)
    vecs[...] = both_pieces(jnp.where(mine, dirs[...], swap_dir_ref[...]))
    own_tiles(left, right, vecs, total, this_core(), True)


def late_kernel(left, right, vecs, total_in, back_in, total, back):
    total[...] = total_in[...]
    back[...] = back_in[...]
    core = this_core()

    @pl.when(jnp.logical_or(core == 1, jnp.logical_not(far_from_other_z())))
    def _():
        own_tiles(left, right, vecs, total, core, False)

    @pl.when(jnp.logical_and(core == 1, far_from_other_z()))
    def _():
        own_tiles(left, right, vecs, total, 1 - core, False)


def kernel_kernel(left, vecs, far_pts_ref, scale_ref, back_ref, kernel_ref, right, total, sq, parts):
    right[...] = right_side(far_pts_ref[...] * scale_ref[:, 0:1])
    total[...] = jnp.zeros_like(total)
    cols = [slice(c * WIDTH, (c + 1) * WIDTH) for c in range(ACROSS)]

    def distances(r, c):
        sq[c % 2] = squares(left[tall_span(r), :], right[:, cols[c]])

    def product(r, c):
        add_columns(total, cols[c], vecs, tall_span(r), (parts[c % 2, 0], parts[c % 2, 1]))

    distances(0, 0)

    def some_rows(r, carry):
        for c in range(ACROSS):
            if c + 1 < ACROSS:
                distances(r, c + 1)
            else:
                distances(jnp.minimum(r + 1, BLOCK // HEIGHT - 1), 0)
            kernel = matern(sq[c % 2])
            kernel_ref[tall_span(r), cols[c]] = kernel
            parts[c % 2, 0], parts[c % 2, 1] = halves(kernel)
            if c > 0:
                product(r, c - 1)
        product(r, ACROSS - 1)
        return carry

    lax.fori_loop(0, BLOCK // HEIGHT, some_rows, 0)
    back_ref[...] = folded(total[...], SHARE)


def product_kernel(kernel_ref, far_dir_ref, total_ref, own_ref, far_vecs, far_coarse, tall):
    vecs = far_dir_ref[...]
    coarse = vecs.astype(F8).astype(F32)
    fine = ((vecs - coarse) * LOW_SCALE).astype(F8).astype(F32)
    columns = jnp.concatenate([part.astype(F32) for part in pieces(vecs, 2)] + [coarse, fine], 0).T
    far_vecs[...] = columns.astype(BF16)
    far_coarse[...] = columns.astype(F8)
    from_head = lax.broadcasted_iota(jnp.int32, (TILE, 128), 1) < 2 * RHS

    def some_rows(r, carry):
        kernel = kernel_ref[span(r), :]
        head = kernel.astype(BF16)
        rest = ((kernel - head.astype(F32)) * REST_SCALE).astype(F8)
        tall[span(r), :] = jnp.where(
            from_head,
            jnp.dot(head, far_vecs[...], preferred_element_type=F32),
            jnp.dot(rest, far_coarse[...], preferred_element_type=F32),
        )
        return carry

    lax.fori_loop(0, STEPS, some_rows, 0)
    wide = tall[...].T
    product = folded(wide[: 2 * RHS], SHARE)
    low = (wide[2 * RHS : 3 * RHS] + wide[3 * RHS :] * (1.0 / LOW_SCALE)) * (SHARE / REST_SCALE)
    own_ref[...] = (product + low) + folded(total_ref[...], 4.0 * SHARE)


def sums_kernel(
    part_ref, other_ref, dir_ref, swap_dir_ref, res_ref, swap_res_ref, product_ref, sums_ref
):
    mine = handles_own_block()
    vecs = jnp.where(mine, dir_ref[...], swap_dir_ref[...])
    res = jnp.where(mine, res_ref[...], swap_res_ref[...])
    product = part_ref[...] + other_ref[...]
    product_ref[...] = product
    image = product + NOISE * vecs
    lane = lax.broadcasted_iota(jnp.int32, (RHS, 128), 1)
    table = jnp.zeros((RHS, 128), F32)
    for i, (a, b) in enumerate(((res, res), (vecs, image), (res, image), (image, image))):
        table = jnp.where(lane == i, jnp.sum(a * b, 1, keepdims=True), table)
    table = jnp.concatenate([table, jnp.zeros((128 - RHS, 128), F32)], 0).T
    row = jnp.concatenate([table[i : i + 1, :RHS] for i in range(4)], 1)
    sums_ref[...] = jnp.broadcast_to(row[None], sums_ref.shape)


def update_kernel(
    sums_ref, active_ref, image_ref, other_ref, dir_ref, res_ref, sol_ref,
    sol_out, res_out, dir_out, sol_next, res_next, dir_next, sent,
):
    row = jnp.sum(sums_ref[...], 0)
    table = jnp.concatenate([row[:, i * RHS : (i + 1) * RHS] for i in range(4)], 0)
    table = jnp.concatenate([table, jnp.zeros((4, RHS), F32)], 0)
    table = jnp.concatenate([table, jnp.zeros((8, 128 - RHS), F32)], 1)
    table = jnp.concatenate([table, jnp.zeros((120, 128), F32)], 0).T
    norm_old, curvature = table[:RHS, 0:1], table[:RHS, 1:2]
    res_image, image_image = table[:RHS, 2:3], table[:RHS, 3:4]
    active = as_column(active_ref[...])
    alpha = active.astype(F32) * norm_old / curvature
    norm_new = norm_old - 2.0 * alpha * res_image + alpha * alpha * image_image
    ratio = norm_new / norm_old
    mine = handles_own_block()
    copies = []
    for k in range(4):
        rows = slice(k * 8, k * 8 + 8)
        vecs = dir_ref[rows]
        image = jnp.where(mine, image_ref[rows], other_ref[rows]) + NOISE * vecs
        sol_next[rows] = sol_ref[rows] + alpha[rows] * vecs
        after = res_ref[rows] - alpha[rows] * image
        res_next[rows] = after
        dir_next[rows] = jnp.where(active[rows] == 1, after + ratio[rows] * vecs, vecs)
        for n, (source, target) in enumerate(((sol_next, sol_out), (res_next, res_out), (dir_next, dir_out))):
            copies.append(pltpu.make_async_copy(source.at[rows], target.at[rows], sent.at[3 * k + n]))
            copies[-1].start()
    for copy in copies:
        copy.wait()


def permuted(value, change):
    pairs = []
    for index in range(256):
        block, rep = index // 2, index % 2
        to = change(block, block % 2, rep)
        pairs.append((index, to[0] % 128 * 2 + to[1]))
    return lax.ppermute(value, AXES, pairs)


def to_partner(block, core, rep):
    if core == rep:
        to = (block + 32, rep)
    else:
        to = (block - 32 - 2 * rep, rep)
    if block % 32 == 0:
        to = (block - 34, 1) if rep == 0 else (block + 32, 0)
    return to


def to_home(block, core, rep):
    if core == rep:
        return block - 32, rep
    return block + 31 + 4 * rep, 1 - rep


def swap_core(block, core, rep):
    return block ^ 1, rep


def swap_rep(block, core, rep):
    return block, 1 - rep


def over_chips(value):
    def hops(k):
        x, z, y = k % 4, k // 4 % 8, k // 32
        return -(min(x, 4 - x) + min(y, 4 - y) + min(z, 8 - z)), -k

    groups = [[k // 2 * 4 + core * 2 + k % 2 for k in sorted(range(128), key=hops)] for core in range(2)]
    return lax.all_to_all(value, AXES, 0, 0, axis_index_groups=groups)


def call(kernel, outs, ins, scratch=(), name=None, out_space=pltpu.VMEM):
    vmem = pl.BlockSpec(memory_space=pltpu.VMEM)
    hbm = pl.BlockSpec(memory_space=pltpu.HBM)
    run = pl.pallas_call(
        kernel,
        out_shape=tuple(jax.ShapeDtypeStruct(*(out if isinstance(out[0], tuple) else (out, F32))) for out in outs),
        in_specs=[hbm if i == "h" else vmem for i in ins],
        out_specs=(pl.BlockSpec(memory_space=out_space),) * len(outs),
        scratch_shapes=scratch,
        compiler_params=pltpu.CompilerParams(vmem_limit_bytes=28 * 2**20),
        name=name,
    )

    def placed(*args):
        return run(*(pltpu.with_memory_space_constraint(a, pltpu.HBM) if i == "h" else a for i, a in zip(ins, args)))

    return placed


def on_device(points, inv_length, direction, residual, solution, active):
    lengths = inv_length.reshape(1, DIM)
    far_pts = permuted(points, to_partner)
    swap_pts = permuted(points, swap_core)
    swap_dir = permuted(direction, swap_core)
    swap_res = permuted(residual, swap_core)
    whole = (RHS, BLOCK)
    left_shape, right_shape = ((BLOCK, DEPTH), BF16), ((DEPTH, BLOCK), BF16)
    vecs_shape, total_shape = ((2 * RHS, BLOCK), BF16), ((2 * RHS, BLOCK), F32)
    left, right, vecs, total, scale = call(
        start_kernel,
        [left_shape, right_shape, vecs_shape, total_shape, (DIM, 128)],
        "hvhhv",
        [
            pltpu.VMEM(whole, F32),
            pltpu.VMEM(whole, F32),
            pltpu.VMEM((1, DIM), F32),
            pltpu.SemaphoreType.DMA((9,)),
        ],
        "own_start",
    )(points, swap_pts, lengths, direction, swap_dir)
    later, scale = lax.optimization_barrier((direction, scale))
    far_dir = permuted(later, to_partner)
    back, kernel = call(
        kernel_kernel,
        [whole, (BLOCK, BLOCK)],
        "vvvv",
        [
            pltpu.VMEM(*right_shape),
            pltpu.VMEM(*total_shape),
            pltpu.VMEM((2, HEIGHT, WIDTH), F32),
            pltpu.VMEM((2, 2, HEIGHT, WIDTH), BF16),
        ],
        "cross_kernel",
    )(left, vecs, far_pts, scale)
    total, back = call(late_kernel, [total_shape, whole], "vvvvv", name="own_late")(
        left, right, vecs, total, back
    )
    back = permuted(back, to_home)
    tall = (BLOCK, 128)
    (own,) = call(
        product_kernel,
        [whole],
        "vvv",
        [pltpu.VMEM(tall, BF16), pltpu.VMEM(tall, F8), pltpu.VMEM(tall, F32)],
        "cross_product",
    )(kernel, far_dir, total)
    part = own + back
    other = permuted(part, swap_core)
    product, sums = call(sums_kernel, [whole, (128, 1, 128)], "vvvvvv", name="sums")(
        part, other, direction, swap_dir, residual, swap_res
    )
    twin = permuted(product, swap_rep)
    return call(
        update_kernel,
        [whole] * 3,
        "vvvvvvv",
        [pltpu.VMEM(whole, F32)] * 3 + [pltpu.SemaphoreType.DMA((12,))],
        "update",
        pltpu.HBM,
    )(
        over_chips(sums), active.reshape(1, RHS), product, twin, direction, residual, solution
    )


def solution(mesh):
    placed = (P(None, "blk"), P(), P(None, "blk"), P(None, "blk"), P(None, "blk"), P())
    return jax.shard_map(
        on_device,
        mesh=mesh,
        in_specs=placed,
        out_specs=(P(None, "blk"), P(None, "blk"), P(None, "blk")),
        check_vma=False,
    )
```

```python
import functools
import math

import jax
import jax.numpy as jnp
from jax import lax
from jax.experimental import pallas as pl
from jax.experimental.pallas import tpu as pltpu
from jax.sharding import PartitionSpec as P

F32, BF16, F8 = jnp.float32, jnp.bfloat16, jnp.float8_e4m3fn
ROOT_FIVE = math.sqrt(5.0)
LOG2_E = 1.4426950408889634
SCALE = ROOT_FIVE * LOG2_E
SHARE = 1.0 / (3.0 * LOG2_E * LOG2_E)
NOISE = 0.5
BLOCK = 2048
DIM = 32
RHS = 32
TILE = 512
STEPS = BLOCK // TILE
WIDTH = 256
HEIGHT = 1024
ACROSS = BLOCK // WIDTH
REST_SCALE = 2.0**14
LOW_SCALE = 2.0**4
DEPTH = 256
AXES = ("blk", "rep")
NT = (((1,), (1,)), ((), ()))


def pieces(value, count):
    out = []
    for _ in range(count):
        head = value.astype(BF16)
        out.append(head)
        value = value - head.astype(F32)
    return out


def norm_rows(points):
    return [part.astype(F32) for part in pieces(jnp.sum(points * points, 0, keepdims=True), 3)]


def left_side(points):
    n = points.shape[1]
    p = [(-2.0 * part.astype(F32)).astype(BF16) for part in pieces(points, 3)]
    m = norm_rows(points)
    row = lax.broadcasted_iota(jnp.int32, (16, n), 0)
    tail = jnp.where(row < 6, 1.0, 0.0)
    for i in range(3):
        tail = jnp.where(row == i, m[i], tail)
    rest = jnp.zeros((DEPTH - 6 * DIM - 16, n), BF16)
    return jnp.concatenate([p[0], p[0], p[1], p[1], p[0], p[2], tail.astype(BF16), rest], 0)


def right_side(points):
    n = points.shape[1]
    p = pieces(points, 3)
    m = norm_rows(points)
    row = lax.broadcasted_iota(jnp.int32, (16, n), 0)
    tail = jnp.where(row < 3, 1.0, 0.0)
    for i in range(3):
        tail = jnp.where(row == 3 + i, m[i], tail)
    rest = jnp.zeros((DEPTH - 6 * DIM - 16, n), BF16)
    return jnp.concatenate([p[0], p[1], p[0], p[1], p[2], p[0], tail.astype(BF16), rest], 0)


def both_pieces(vectors):
    return jnp.concatenate(pieces(vectors, 2), 0)


def squares(left, right):
    return jnp.maximum(jnp.dot(left, right, preferred_element_type=F32), 1e-30)


def matern(sq):
    dist = sq * lax.rsqrt(sq)
    return (dist * (dist + 3.0 * LOG2_E) + 3.0 * LOG2_E * LOG2_E) * jnp.exp2(-dist)


def halves(kernel):
    head = kernel.astype(BF16)
    return head, (kernel - head.astype(F32)).astype(BF16)


def add_rows(total, rows, vecs, cols, kernel):
    head, rest = kernel
    total[:, rows] += lax.dot_general(vecs[:, cols], head, NT, preferred_element_type=F32)
    total[:RHS, rows] += lax.dot_general(vecs[:RHS, cols], rest, NT, preferred_element_type=F32)


def add_columns(total, cols, vecs, rows, kernel):
    head, rest = kernel
    total[:, cols] += jnp.dot(vecs[:, rows], head, preferred_element_type=F32)
    total[:RHS, cols] += jnp.dot(vecs[:RHS, rows], rest, preferred_element_type=F32)


def span(index):
    return pl.ds(pl.multiple_of(index * TILE, TILE), TILE)


def tall_span(index):
    return pl.ds(pl.multiple_of(index * HEIGHT, HEIGHT), HEIGHT)


def as_column(row):
    n = row.shape[1]
    square = lax.broadcasted_iota(jnp.int32, (n, n), 0) == lax.broadcasted_iota(jnp.int32, (n, n), 1)
    return jnp.sum(jnp.where(square, row, jnp.zeros_like(row)), 1, keepdims=True)


def folded(total, scale):
    return (total[:RHS] + total[RHS:]) * scale


def handles_own_block():
    return lax.rem(lax.axis_index("blk"), 2) == lax.axis_index("rep")


def this_core():
    return lax.rem(lax.axis_index("blk"), 2)


def far_from_other_z():
    return jnp.logical_and(lax.rem(lax.axis_index("blk"), 4) >= 2, lax.axis_index("rep") == 1)


def own_tiles(left, right, vecs, total, half, first):
    def diagonal(i):
        rows = span(i)
        add_columns(total, rows, vecs, rows, halves(matern(squares(left[rows, :], right[:, rows]))))

    def pair(i, j):
        rows, cols = span(i), span(j)
        kernel = halves(matern(squares(left[rows, :], right[:, cols])))
        add_rows(total, rows, vecs, cols, kernel)
        add_columns(total, cols, vecs, rows, kernel)

    i = half * (STEPS // 2)
    if first:
        diagonal(i)
        pair(i, i + 1)
    else:
        diagonal(i + 1)
        pair(i + 1, lax.rem(i + 2, STEPS))
        pair(half, half + STEPS // 2)


def start_kernel(
    pts_ref, swap_pts_ref, len_ref, dir_ref, swap_dir_ref,
    left, right, vecs, total, scale_ref, pts, dirs, lengths, arrived,
):
    copies = [pltpu.make_async_copy(len_ref, lengths, arrived.at[8])]
    for n, (source, target) in enumerate(((pts_ref, pts), (dir_ref, dirs))):
        for k in range(4):
            rows = slice(k * 8, k * 8 + 8)
            copies.append(pltpu.make_async_copy(source.at[rows], target.at[rows], arrived.at[4 * n + k]))
    for copy in copies:
        copy.start()
    mine = handles_own_block()
    total[...] = jnp.zeros_like(total)
    for copy in copies:
        copy.wait()
    scale = as_column(lengths[...]) * SCALE
    scale_ref[...] = jnp.broadcast_to(scale, scale_ref.shape)
    points = jnp.where(mine, pts[...], swap_pts_ref[...]) * scale
    left[...] = left_side(points).T
    right[...] = right_side(points)
    vecs[...] = both_pieces(jnp.where(mine, dirs[...], swap_dir_ref[...]))
    own_tiles(left, right, vecs, total, this_core(), True)


def own_rest(left, right, vecs, total):
    core = this_core()

    @pl.when(jnp.logical_or(core == 1, jnp.logical_not(far_from_other_z())))
    def _():
        own_tiles(left, right, vecs, total, core, False)

    @pl.when(jnp.logical_and(core == 1, far_from_other_z()))
    def _():
        own_tiles(left, right, vecs, total, 1 - core, False)


def kernel_kernel(
    left, vecs, far_pts_ref, scale_ref, own_right, own_in, back_ref, kernel_ref, own_total, right, total, sq, parts
):
    right[...] = right_side(far_pts_ref[...] * scale_ref[:, 0:1])
    total[...] = jnp.zeros_like(total)
    cols = [slice(c * WIDTH, (c + 1) * WIDTH) for c in range(ACROSS)]

    def distances(r, c):
        sq[c % 2] = squares(left[tall_span(r), :], right[:, cols[c]])

    def product(r, c):
        add_columns(total, cols[c], vecs, tall_span(r), (parts[c % 2, 0], parts[c % 2, 1]))

    distances(0, 0)

    def some_rows(r, carry):
        for c in range(ACROSS):
            if c + 1 < ACROSS:
                distances(r, c + 1)
            else:
                distances(jnp.minimum(r + 1, BLOCK // HEIGHT - 1), 0)
            kernel = matern(sq[c % 2])
            kernel_ref[tall_span(r), cols[c]] = kernel
            parts[c % 2, 0], parts[c % 2, 1] = halves(kernel)
            if c > 0:
                product(r, c - 1)
        product(r, ACROSS - 1)
        return carry

    lax.fori_loop(0, BLOCK // HEIGHT, some_rows, 0)
    back_ref[...] = folded(total[...], SHARE)
    own_total[...] = own_in[...]
    own_rest(left, own_right, vecs, own_total)


def product_kernel(kernel_ref, far_dir_ref, total_ref, own_ref, far_vecs, far_coarse, tall):
    vecs = far_dir_ref[...]
    coarse = vecs.astype(F8).astype(F32)
    fine = ((vecs - coarse) * LOW_SCALE).astype(F8).astype(F32)
    columns = jnp.concatenate([part.astype(F32) for part in pieces(vecs, 2)] + [coarse, fine], 0).T
    far_vecs[...] = columns.astype(BF16)
    far_coarse[...] = columns.astype(F8)
    from_head = lax.broadcasted_iota(jnp.int32, (TILE, 128), 1) < 2 * RHS

    def some_rows(r, carry):
        kernel = kernel_ref[span(r), :]
        head = kernel.astype(BF16)
        rest = ((kernel - head.astype(F32)) * REST_SCALE).astype(F8)
        tall[span(r), :] = jnp.where(
            from_head,
            jnp.dot(head, far_vecs[...], preferred_element_type=F32),
            jnp.dot(rest, far_coarse[...], preferred_element_type=F32),
        )
        return carry

    lax.fori_loop(0, STEPS, some_rows, 0)
    wide = tall[...].T
    product = folded(wide[: 2 * RHS], SHARE)
    low = (wide[2 * RHS : 3 * RHS] + wide[3 * RHS :] * (1.0 / LOW_SCALE)) * (SHARE / REST_SCALE)
    own_ref[...] = (product + low) + folded(total_ref[...], 4.0 * SHARE)


def sums_kernel(
    part_ref, other_ref, dir_ref, swap_dir_ref, res_ref, swap_res_ref, product_ref, sums_ref
):
    mine = handles_own_block()
    vecs = jnp.where(mine, dir_ref[...], swap_dir_ref[...])
    res = jnp.where(mine, res_ref[...], swap_res_ref[...])
    product = part_ref[...] + other_ref[...]
    product_ref[...] = product
    image = product + NOISE * vecs
    lane = lax.broadcasted_iota(jnp.int32, (RHS, 128), 1)
    table = jnp.zeros((RHS, 128), F32)
    for i, (a, b) in enumerate(((res, res), (vecs, image), (res, image), (image, image))):
        table = jnp.where(lane == i, jnp.sum(a * b, 1, keepdims=True), table)
    table = jnp.concatenate([table, jnp.zeros((128 - RHS, 128), F32)], 0).T
    row = jnp.concatenate([table[i : i + 1, :RHS] for i in range(4)], 1)
    sums_ref[...] = jnp.broadcast_to(row[None], sums_ref.shape)


def update_kernel(
    sums_ref, active_ref, image_ref, other_ref, dir_ref, res_ref, sol_ref,
    sol_out, res_out, dir_out, sol_next, res_next, dir_next, sent,
):
    row = jnp.sum(sums_ref[...], 0)
    table = jnp.concatenate([row[:, i * RHS : (i + 1) * RHS] for i in range(4)], 0)
    table = jnp.concatenate([table, jnp.zeros((4, RHS), F32)], 0)
    table = jnp.concatenate([table, jnp.zeros((8, 128 - RHS), F32)], 1)
    table = jnp.concatenate([table, jnp.zeros((120, 128), F32)], 0).T
    norm_old, curvature = table[:RHS, 0:1], table[:RHS, 1:2]
    res_image, image_image = table[:RHS, 2:3], table[:RHS, 3:4]
    active = as_column(active_ref[...])
    alpha = active.astype(F32) * norm_old / curvature
    norm_new = norm_old - 2.0 * alpha * res_image + alpha * alpha * image_image
    ratio = norm_new / norm_old
    mine = handles_own_block()
    copies = []
    for k in range(4):
        rows = slice(k * 8, k * 8 + 8)
        vecs = dir_ref[rows]
        image = jnp.where(mine, image_ref[rows], other_ref[rows]) + NOISE * vecs
        sol_next[rows] = sol_ref[rows] + alpha[rows] * vecs
        after = res_ref[rows] - alpha[rows] * image
        res_next[rows] = after
        dir_next[rows] = jnp.where(active[rows] == 1, after + ratio[rows] * vecs, vecs)
        for n, (source, target) in enumerate(((sol_next, sol_out), (res_next, res_out), (dir_next, dir_out))):
            copies.append(pltpu.make_async_copy(source.at[rows], target.at[rows], sent.at[3 * k + n]))
            copies[-1].start()
    for copy in copies:
        copy.wait()


def permuted(value, change):
    pairs = []
    for index in range(256):
        block, rep = index // 2, index % 2
        to = change(block, block % 2, rep)
        pairs.append((index, to[0] % 128 * 2 + to[1]))
    return lax.ppermute(value, AXES, pairs)


def to_partner(block, core, rep):
    if core == rep:
        to = (block + 32, rep)
    else:
        to = (block - 32 - 2 * rep, rep)
    if block % 32 == 0:
        to = (block - 34, 1) if rep == 0 else (block + 32, 0)
    return to


def to_home(block, core, rep):
    if core == rep:
        return block - 32, rep
    return block + 31 + 4 * rep, 1 - rep


def swap_core(block, core, rep):
    return block ^ 1, rep


def swap_rep(block, core, rep):
    return block, 1 - rep


def over_chips(value):
    def hops(k):
        x, z, y = k % 4, k // 4 % 8, k // 32
        return -(min(x, 4 - x) + min(y, 4 - y) + min(z, 8 - z)), -k

    groups = [[k // 2 * 4 + core * 2 + k % 2 for k in sorted(range(128), key=hops)] for core in range(2)]
    return lax.all_to_all(value, AXES, 0, 0, axis_index_groups=groups)


def call(kernel, outs, ins, scratch=(), name=None, out_space=pltpu.VMEM):
    vmem = pl.BlockSpec(memory_space=pltpu.VMEM)
    hbm = pl.BlockSpec(memory_space=pltpu.HBM)
    run = pl.pallas_call(
        kernel,
        out_shape=tuple(jax.ShapeDtypeStruct(*(out if isinstance(out[0], tuple) else (out, F32))) for out in outs),
        in_specs=[hbm if i == "h" else vmem for i in ins],
        out_specs=(pl.BlockSpec(memory_space=out_space),) * len(outs),
        scratch_shapes=scratch,
        compiler_params=pltpu.CompilerParams(vmem_limit_bytes=28 * 2**20),
        name=name,
    )

    def placed(*args):
        return run(*(pltpu.with_memory_space_constraint(a, pltpu.HBM) if i == "h" else a for i, a in zip(ins, args)))

    return placed


def on_device(points, inv_length, direction, residual, solution, active):
    lengths = inv_length.reshape(1, DIM)
    far_pts = permuted(points, to_partner)
    swap_pts = permuted(points, swap_core)
    swap_dir = permuted(direction, swap_core)
    swap_res = permuted(residual, swap_core)
    whole = (RHS, BLOCK)
    left_shape, right_shape = ((BLOCK, DEPTH), BF16), ((DEPTH, BLOCK), BF16)
    vecs_shape, total_shape = ((2 * RHS, BLOCK), BF16), ((2 * RHS, BLOCK), F32)
    left, right, vecs, total, scale = call(
        start_kernel,
        [left_shape, right_shape, vecs_shape, total_shape, (DIM, 128)],
        "hvhhv",
        [
            pltpu.VMEM(whole, F32),
            pltpu.VMEM(whole, F32),
            pltpu.VMEM((1, DIM), F32),
            pltpu.SemaphoreType.DMA((9,)),
        ],
        "own_start",
    )(points, swap_pts, lengths, direction, swap_dir)
    later, scale = lax.optimization_barrier((direction, scale))
    far_dir = permuted(later, to_partner)
    back, kernel, total = call(
        kernel_kernel,
        [whole, (BLOCK, BLOCK), total_shape],
        "vvvvvv",
        [
            pltpu.VMEM(*right_shape),
            pltpu.VMEM(*total_shape),
            pltpu.VMEM((2, HEIGHT, WIDTH), F32),
            pltpu.VMEM((2, 2, HEIGHT, WIDTH), BF16),
        ],
        "cross_kernel",
    )(left, vecs, far_pts, scale, right, total)
    back = permuted(back, to_home)
    tall = (BLOCK, 128)
    (own,) = call(
        product_kernel,
        [whole],
        "vvv",
        [pltpu.VMEM(tall, BF16), pltpu.VMEM(tall, F8), pltpu.VMEM(tall, F32)],
        "cross_product",
    )(kernel, far_dir, total)
    part = own + back
    other = permuted(part, swap_core)
    product, sums = call(sums_kernel, [whole, (128, 1, 128)], "vvvvvv", name="sums")(
        part, other, direction, swap_dir, residual, swap_res
    )
    twin = permuted(product, swap_rep)
    return call(
        update_kernel,
        [whole] * 3,
        "vvvvvvv",
        [pltpu.VMEM(whole, F32)] * 3 + [pltpu.SemaphoreType.DMA((12,))],
        "update",
        pltpu.HBM,
    )(
        over_chips(sums), active.reshape(1, RHS), product, twin, direction, residual, solution
    )


def solution(mesh):
    placed = (P(None, "blk"), P(), P(None, "blk"), P(None, "blk"), P(None, "blk"), P())
    return jax.shard_map(
        on_device,
        mesh=mesh,
        in_specs=placed,
        out_specs=(P(None, "blk"), P(None, "blk"), P(None, "blk")),
        check_vma=False,
    )
```
